128 devices in a mesh: segment: 8 (over x, core), mp: 16 (over z, y).
Axes of the slice: x: 4, y: 4, z: 4, core: 2. Of those that a mesh axis runs over, the one named last changes fastest.
Arguments:
- token_ids: int32 [128], replicated, may hold values from 0 to 128255
- teacher_seeds: int32 [8], P('segment'), may hold values from 0 to 16777215
- student_seeds: int32 [8], P('segment'), may hold values from 0 to 16777215
- teacher_gain: bfloat16 [8, 16384], P('segment', 'mp'), may hold values from 0.099609375 to 1.8984375
- student_gain: bfloat16 [8, 16384], P('segment'), may hold values from 0.099609375 to 1.8984375
Outputs:
- losses: float32 [8], P('segment')
- grad_up: float32 [8, 16384, 128], P('segment', 'mp')
- grad_down: float32 [8, 16384, 128], P('segment', 'mp')
The draws below stay inside these ranges and needn't reach their ends.
All inputs are finite; a program needn't handle non-finite values.
Results may differ from the reference program's by a relative error of at most 0.029.
Values may be sent and summed in bfloat16 or wider, within the bound.
No kernel may reach another device: no remote copies, remote signals or barrier semaphores. Data moves between devices by JAX's collectives and lax.ppermute only.
A program may use at most 64 MiB of HBM per device.

```python
import math
import jax
import jax.numpy as jnp
import numpy as np
from jax import lax

D = 16384
VOCAB = 128256
R = 128
MB_TOK = 128
LAYERS = 8


def with_ends(entries, key, low, largest):
    index_at = [jax.random.randint(jax.random.fold_in(key, axis), (), 0, length) for axis, length in enumerate(entries.shape)]
    widest = entries.shape.index(max(entries.shape))
    next_to = index_at[:widest] + [(index_at[widest] + 1) % entries.shape[widest]] + index_at[widest + 1:]
    return entries.at[tuple(index_at)].set(low).at[tuple(next_to)].set(largest)


def ranked_wide(own_key, extent, count, slope):
    loads = [min(1 << octave, count + 1 - (1 << octave)) * (1 << 20) // math.isqrt((1 << octave) ** slope) + 1 for octave in range((count + 1).bit_length()) if 1 << octave <= count]
    deviation = 1 + sum(loads) // (1 << 30)
    table = np.cumsum(np.array([max(1, weight // deviation) for weight in loads]))
    ticket = jax.random.randint(jax.random.fold_in(own_key, 1), extent, 0, int(table[len(loads) - 1]))
    start = jnp.left_shift(1, jnp.searchsorted(jnp.asarray(table, jnp.int32), ticket, side="right").astype(jnp.int32))
    grade = start - 1 + jax.random.randint(jax.random.fold_in(own_key, 4), extent, 0, 1 << 30) % jnp.minimum(start, count + 1 - start)
    return jax.random.permutation(jax.random.fold_in(own_key, 2), count)[grade].astype(jnp.int32)


def setup_inputs(seed: int = 0) -> dict:
    key_list = jax.random.split(jax.random.key(seed), 6)
    return {
        "token_ids": with_ends(ranked_wide(key_list[0], (MB_TOK,), VOCAB, 2), jax.random.fold_in(key_list[0], 3), 0, VOCAB - 1).astype(jnp.int32),
        "teacher_seeds": with_ends(jax.random.randint(key_list[1], (LAYERS,), 0, 16777216), jax.random.fold_in(key_list[1], 1), 0, 16777215).astype(jnp.int32),
        "student_seeds": with_ends(jax.random.randint(key_list[2], (LAYERS,), 0, 16777216), jax.random.fold_in(key_list[2], 1), 0, 16777215).astype(jnp.int32),
        "teacher_gain": jnp.clip(1.0 + 0.18 * jax.random.normal(key_list[3], (LAYERS, D), jnp.float32), 0.099609375, 1.8984375).astype(jnp.bfloat16),
        "student_gain": jnp.clip(1.0 + 0.18 * jax.random.normal(key_list[4], (LAYERS, D), jnp.float32), 0.099609375, 1.8984375).astype(jnp.bfloat16),
    }


EPSILON = 1e-05
EMBED_KEY = 7919

def scramble(mixed_bits):
    multiplier = jnp.int32(73244475)
    mixed_bits = jnp.bitwise_xor(mixed_bits, lax.shift_right_logical(mixed_bits, jnp.int32(16)))
    mixed_bits = mixed_bits * multiplier
    mixed_bits = jnp.bitwise_xor(mixed_bits, lax.shift_right_logical(mixed_bits, jnp.int32(16)))
    mixed_bits = mixed_bits * multiplier
    mixed_bits = jnp.bitwise_xor(mixed_bits, lax.shift_right_logical(mixed_bits, jnp.int32(16)))
    return mixed_bits

def uniform_bits(layer_seed, row_index, col_index):
    mixed_bits = layer_seed * jnp.int32(1000003) + row_index * jnp.int32(16411) + col_index
    return lax.shift_right_logical(scramble(scramble(mixed_bits)), jnp.int32(8))

def hashed(layer_seed, row_index, col_index, magnitude):
    bits_value = uniform_bits(layer_seed, row_index, col_index)
    return (bits_value.astype(jnp.float32) * (2.0 / 16777216.0) - 1.0) * magnitude

def ternary(layer_seed, row_index, col_index, magnitude):
    bits_value = uniform_bits(layer_seed, row_index, col_index)
    return (jnp.remainder(bits_value, jnp.int32(3)) - jnp.int32(1)).astype(jnp.float32) * magnitude

def teacher_layer(stream, layer_seed, norm_gain):
    block_width = D // 8
    row_index = jnp.arange(D, dtype=jnp.int32)
    scaled_in = (stream.astype(jnp.float32) * norm_gain.astype(jnp.float32)).astype(jnp.bfloat16)
    mean_sq = lax.optimization_barrier(jnp.mean(jnp.square(stream.astype(jnp.float32)), axis=1, keepdims=True))

    def column_block(block_id):
        col_index = block_id * block_width + jnp.arange(block_width, dtype=jnp.int32)
        weight_block = hashed(layer_seed, row_index[:, None], col_index[None, :], math.sqrt(3.0 / D)).astype(jnp.bfloat16)
        return jnp.dot(scaled_in, weight_block, preferred_element_type=jnp.float32)
    blocks = lax.map(column_block, jnp.arange(8, dtype=jnp.int32))
    update = jnp.transpose(blocks, (1, 0, 2)).reshape(stream.shape[0], D)
    layer_out = (stream.astype(jnp.float32) + update * lax.rsqrt(mean_sq + EPSILON)).astype(jnp.bfloat16)
    return (layer_out, mean_sq)

def student_block(stream, target, mean_sq, layer_seed, norm_gain):
    row_index = jnp.arange(D, dtype=jnp.int32)[:, None]
    rank_index = jnp.arange(R, dtype=jnp.int32)[None, :]
    up_weight = ternary(layer_seed, row_index, rank_index, math.sqrt(1.5 / D)).astype(jnp.bfloat16)
    down_weight = ternary(layer_seed, row_index, rank_index + R, math.sqrt(1.5 / R)).astype(jnp.bfloat16)
    hidden_in = stream.astype(jnp.float32)
    normed = (hidden_in * lax.rsqrt(mean_sq + EPSILON) * norm_gain.astype(jnp.float32)).astype(jnp.bfloat16)
    pre_act = jnp.dot(normed, up_weight, preferred_element_type=jnp.float32)
    rectified = jnp.maximum(pre_act, 0.0)
    squared = (rectified * rectified).astype(jnp.bfloat16)
    student_out = hidden_in + jnp.dot(squared, down_weight.T, preferred_element_type=jnp.float32)
    error = student_out - target.astype(jnp.float32)
    layer_loss = jnp.mean(error * error)
    scaled_error = (error / MB_TOK).astype(jnp.bfloat16)
    grad_down = jnp.dot(scaled_error.T, squared, preferred_element_type=jnp.float32)
    back = jnp.dot(scaled_error, down_weight, preferred_element_type=jnp.float32)
    back_pre = (back * 2.0 * rectified).astype(jnp.bfloat16)
    grad_up = jnp.dot(normed.T, back_pre, preferred_element_type=jnp.float32)
    return (layer_loss, grad_up, grad_down)

def reference(token_ids, teacher_seeds, student_seeds, teacher_gain, student_gain):
    col_index = jnp.arange(D, dtype=jnp.int32)
    stream = hashed(jnp.int32(EMBED_KEY), token_ids[:, None].astype(jnp.int32), col_index[None, :], math.sqrt(3.0)).astype(jnp.bfloat16)
    losses = []
    up_grads = []
    down_grads = []
    for layer_id in range(LAYERS):
        layer_out, mean_sq = teacher_layer(stream, teacher_seeds[layer_id], teacher_gain[layer_id])
        layer_loss, grad_up, grad_down = student_block(stream, layer_out, mean_sq, student_seeds[layer_id], student_gain[layer_id])
        losses.append(layer_loss)
        up_grads.append(grad_up)
        down_grads.append(grad_down)
        stream = layer_out
    return (jnp.stack(losses), jnp.stack(up_grads), jnp.stack(down_grads))
```

```python
import math

import jax
import jax.numpy as jnp
import numpy as np
from jax import lax
from jax.experimental import pallas as pl
from jax.experimental.pallas import tpu as pltpu
from jax.sharding import PartitionSpec as P

D = 16384
R = 128
TOK = 128
LAYERS = 8
SEG = 8
MP = 16
WIDTH = D // MP
PIECE = WIDTH // SEG
ROWS = TOK + 16
EPSILON = 1e-05
EMBED_KEY = 7919
BF = jnp.bfloat16
F32 = jnp.float32


def wrapped(value):
    value &= 0xFFFFFFFF
    return np.int32(value - (1 << 32) if value >> 31 else value)


MULT = wrapped(73244475)
MULT_SQ = wrapped(73244475 * 73244475)


def fold(bits):
    return jnp.bitwise_xor(bits, lax.shift_right_logical(bits, jnp.int32(16)))


def uniform_bits(mixed_bits):
    mixed_bits = fold(mixed_bits) * MULT
    mixed_bits = fold(mixed_bits) * MULT_SQ
    mixed_bits = fold(mixed_bits) * MULT
    return lax.shift_right_logical(fold(mixed_bits), jnp.int32(8))


def hashed(mixed_bits, magnitude):
    return uniform_bits(mixed_bits).astype(F32) * np.float32(magnitude * 2.0 / 16777216.0) - np.float32(magnitude)


def ternary(mixed_bits, magnitude):
    bits = uniform_bits(mixed_bits)
    return (lax.rem(bits, jnp.int32(3)) - jnp.int32(1)).astype(F32) * np.float32(magnitude)


def split_row(row):
    high = row.astype(BF).astype(F32)
    index = lax.broadcasted_iota(jnp.int32, (16, row.shape[1]), 0)
    tile = jnp.where(index == 0, high, jnp.where(index == 1, row - high, 0.0))
    return tile.astype(BF)


def joined_row(tile):
    return jnp.sum(tile.astype(F32), axis=0, keepdims=True)


SMEM = pl.BlockSpec(memory_space=pltpu.SMEM)
VMEM = pl.BlockSpec(memory_space=pltpu.VMEM)


def call(body, name, out_shape, in_specs, flops=0, nbytes=0, limit=48 << 20):
    single = not isinstance(out_shape, (tuple, list))
    return pl.pallas_call(
        body,
        out_shape=out_shape,
        in_specs=in_specs,
        out_specs=VMEM if single else tuple(VMEM for _ in out_shape),
        name=name,
        cost_estimate=pl.CostEstimate(flops=flops, bytes_accessed=nbytes, transcendentals=0),
        compiler_params=pltpu.CompilerParams(vmem_limit_bytes=limit),
    )


def sds(shape, dtype):
    return jax.ShapeDtypeStruct(shape, dtype)


def weight_kernel(place, out):
    chunk = 32
    row = lax.broadcasted_iota(jnp.int32, (chunk, WIDTH), 0)
    col = lax.broadcasted_iota(jnp.int32, (chunk, WIDTH), 1)
    base = row * 16411 + col + (place[0] * 1000003 + place[1] * (PIECE * 16411) + place[2] * WIDTH)
    per = PIECE // chunk

    def step(index, carry):
        first = (index // per) * WIDTH + (index % per) * chunk
        start = pl.multiple_of(index * chunk, chunk)
        out[pl.ds(start, chunk), :] = hashed(base + first * 16411, math.sqrt(3.0 / D)).astype(BF)
        return carry

    lax.fori_loop(0, MP * per, step, 0)


def teacher_weight(seed, segment, block):
    return call(
        weight_kernel,
        "weight",
        sds((MP * PIECE, WIDTH), BF),
        [SMEM],
        flops=20 * MP * PIECE * WIDTH,
        nbytes=2 * MP * PIECE * WIDTH,
    )(jnp.stack([seed, segment, block]))


def message(out, stream, gain):
    wide = stream.astype(F32)
    scaled = (wide * gain).astype(BF)
    squares = jnp.sum(wide * wide, axis=1, keepdims=True)
    tile = split_row(jnp.transpose(jnp.broadcast_to(squares, (TOK, TOK)))[:1])
    for index in range(MP):
        out[index, :TOK, :] = scaled
        out[index, TOK:, :] = tile


def first_kernel(place, token, gain, stream_out, message_out):
    col = lax.broadcasted_iota(jnp.int32, (TOK, PIECE), 1) + place[0]
    mixed = token[...] * 16411 + col + jnp.int32((EMBED_KEY * 1000003) % (1 << 32) - (1 << 32))
    stream = hashed(mixed, math.sqrt(3.0)).astype(BF)
    stream_out[...] = stream
    message(message_out, stream, gain[...])


def update_kernel(own, part_a, part_b, part_c, stream, gain, stream_out, mean_out, message_out):
    total = own[...]
    for part in (part_a, part_b, part_c):
        total = total + part[...].astype(F32)
    squares = joined_row(total[TOK:])
    mean = jnp.transpose(jnp.broadcast_to(squares, (TOK, TOK))) * np.float32(1.0 / D)
    mean_out[...] = mean
    result = (stream[...].astype(F32) + total[:TOK] * lax.rsqrt(mean + EPSILON)).astype(BF)
    stream_out[...] = result
    message(message_out, result, gain[...])


def contract_kernel(place, gathered, weight, own_out, other_out):
    scaled = jnp.concatenate([gathered[index, :TOK, :] for index in range(MP)], axis=1)
    squares = joined_row(gathered[0, TOK:, :])
    for index in range(1, MP):
        squares = squares + joined_row(gathered[index, TOK:, :])
    tile = split_row(squares)
    first = place[0] == 0
    for chunk in range(4):
        part = jnp.dot(scaled, weight[:, chunk * 256 : (chunk + 1) * 256], preferred_element_type=F32)
        left, right = part[:, :PIECE], part[:, PIECE:]
        own_out[chunk, :TOK, :] = jnp.where(first, left, right)
        other_out[chunk, :TOK, :] = jnp.where(first, right, left).astype(BF)
        own_out[chunk, TOK:, :] = tile.astype(F32)
        other_out[chunk, TOK:, :] = tile


def pair_kernel(place, own, other, kept, send_a, send_b, send_c):
    def total(chunk):
        return own[chunk] + other[chunk].astype(F32)

    def packed(chunk):
        both = total(chunk)
        return both[:TOK].astype(BF), split_row(joined_row(both[TOK:]))

    here = place[0]
    kept[...] = total(here)
    for shift, out in ((1, send_a), (2, send_b), (3, send_c)):
        body, tile = packed(lax.rem(here + shift, 4))
        out[:TOK, :] = body
        out[TOK:, :] = tile


CORE = [(i, i ^ 1) for i in range(SEG)]


def along_x(shift):
    return [(i, (i + 2 * shift) % SEG) for i in range(SEG)]


def along_y(shift):
    return [(i, i // 4 * 4 + (i + shift) % 4) for i in range(MP)]


def along_z(shift):
    return [(i, (i + 4 * shift) % MP) for i in range(MP)]


def sum_mp(value):
    for along in (along_y, along_z):
        parts = [lax.ppermute(value, "mp", along(shift)) for shift in (1, 2, 3)]
        value = (value + parts[1]) + (parts[0] + parts[2])
    return value


def student_up_kernel(place, pieces, mean, gain, normed_out, pre_out):
    row = lax.broadcasted_iota(jnp.int32, (PIECE, R), 0)
    rank = lax.broadcasted_iota(jnp.int32, (PIECE, R), 1)
    base = row * 16411 + rank + (place[0] * 1000003 + place[1] * (WIDTH * 16411))
    scale = lax.rsqrt(mean[...] + EPSILON)
    total = jnp.zeros((TOK, R), F32)
    for index in range(SEG):
        up_weight = ternary(base + index * PIECE * 16411, math.sqrt(1.5 / D)).astype(BF)
        columns = slice(index * PIECE, (index + 1) * PIECE)
        normed = (pieces[index, 0].astype(F32) * scale * gain[:, columns].astype(F32)).astype(BF)
        normed_out[:, columns] = normed
        total = total + jnp.dot(normed, up_weight, preferred_element_type=F32)
    pre_out[...] = total


def student_error_kernel(place, pieces, pre, back_out, scaled_out, squared_out):
    row = lax.broadcasted_iota(jnp.int32, (PIECE, R), 0)
    rank = lax.broadcasted_iota(jnp.int32, (PIECE, R), 1)
    base = row * 16411 + rank + (place[0] * 1000003 + place[1] * (WIDTH * 16411) + R)
    rectified = jnp.maximum(pre[...], 0.0)
    squared = (rectified * rectified).astype(BF)
    squared_out[...] = squared
    back = jnp.zeros((TOK, R), F32)
    squares = jnp.zeros((TOK, PIECE), F32)
    for index in range(SEG):
        down_weight = ternary(base + index * PIECE * 16411, math.sqrt(1.5 / R)).astype(BF)
        student = lax.dot_general(squared, down_weight, (((1,), (1,)), ((), ())), preferred_element_type=F32)
        error = pieces[index, 0].astype(F32) + student - pieces[index, 1].astype(F32)
        squares = squares + error * error
        scaled = (error * np.float32(1.0 / TOK)).astype(BF)
        scaled_out[:, index * PIECE : (index + 1) * PIECE] = scaled
        back = back + jnp.dot(scaled, down_weight, preferred_element_type=F32)
    back_out[:TOK, :] = back
    back_out[TOK:, :] = jnp.sum(squares.reshape(TOK // 8, 8, PIECE), axis=0)


def student_grad_kernel(normed, scaled, squared, pre, back, up_out, down_out):
    rectified = jnp.maximum(pre[...], 0.0)
    back_pre = (back[:TOK, :] * 2.0 * rectified).astype(BF)
    over_tokens = (((0,), (0,)), ((), ()))
    up_out[...] = lax.dot_general(normed[...], back_pre, over_tokens, preferred_element_type=F32)
    down_out[...] = lax.dot_general(scaled[...], squared[...], over_tokens, preferred_element_type=F32)


def local(token_ids, teacher_seeds, student_seeds, teacher_gain, student_gain):
    block = lax.axis_index("mp")
    segment = lax.axis_index("segment")
    core = lax.rem(segment, 2)
    column = segment // 2

    gains = teacher_gain.astype(F32).reshape(SEG, 1, PIECE)
    seeds = jnp.broadcast_to(teacher_seeds.astype(F32).reshape(1, 1, 1), (SEG, 1, PIECE))
    layer_facts = lax.all_to_all(
        jnp.concatenate([gains, seeds], axis=1), "segment", split_axis=0, concat_axis=0, tiled=True
    )
    layer_gains = layer_facts[:, 0]
    layer_seeds = layer_facts[:, 1, 0].astype(jnp.int32)

    message_shape = sds((MP, ROWS, PIECE), BF)
    piece_shape = sds((TOK, PIECE), BF)
    stream, outgoing = call(first_kernel, "first", (piece_shape, message_shape), [SMEM, VMEM, VMEM])(
        (block * WIDTH + segment * PIECE).reshape(1), token_ids.reshape(TOK, 1), layer_gains[:1]
    )
    streams, means = [stream], []
    for layer in range(LAYERS):
        weight = teacher_weight(layer_seeds[layer], segment, block)
        gathered = lax.all_to_all(outgoing, "mp", split_axis=0, concat_axis=0, tiled=True)
        own, other = call(
            contract_kernel,
            "contract",
            (sds((4, ROWS, PIECE), F32), sds((4, ROWS, PIECE), BF)),
            [SMEM, VMEM, VMEM],
            flops=2 * TOK * MP * PIECE * WIDTH,
            nbytes=2 * MP * PIECE * WIDTH,
        )(core.reshape(1), gathered, weight)
        other = lax.ppermute(other, "segment", CORE)
        kept, *sends = call(
            pair_kernel,
            "pair",
            (sds((ROWS, PIECE), F32),) + tuple(sds((ROWS, PIECE), BF) for _ in range(3)),
            [SMEM, VMEM, VMEM],
        )(column.reshape(1), own, other)
        parts = [lax.ppermute(send, "segment", along_x(shift)) for shift, send in zip((1, 2, 3), sends)]
        next_gain = layer_gains[min(layer + 1, LAYERS - 1)].reshape(1, PIECE)
        stream, mean, outgoing = call(
            update_kernel, "update", (piece_shape, sds((TOK, PIECE), F32), message_shape), [VMEM] * 6
        )(kept, *parts, stream, next_gain)
        streams.append(stream)
        means.append(mean)

    pairs = jnp.stack([jnp.stack([streams[layer], streams[layer + 1]]) for layer in range(LAYERS)])
    pieces = lax.all_to_all(pairs, "segment", split_axis=0, concat_axis=0, tiled=True)
    mean = lax.dynamic_index_in_dim(jnp.stack(means), segment, 0, False)
    place = jnp.stack([student_seeds[0], block])
    gain = lax.dynamic_slice_in_dim(student_gain, block * WIDTH, WIDTH, 1)
    normed, pre = call(
        student_up_kernel, "student_up", (sds((TOK, WIDTH), BF), sds((TOK, R), F32)), [SMEM, VMEM, VMEM, VMEM]
    )(place, pieces, mean, gain)
    pre = sum_mp(pre)
    back, scaled, squared = call(
        student_error_kernel,
        "student_error",
        (sds((TOK + 8, R), F32), sds((TOK, WIDTH), BF), sds((TOK, R), BF)),
        [SMEM, VMEM, VMEM],
    )(place, pieces, pre)
    back = sum_mp(back)
    grad_up, grad_down = call(
        student_grad_kernel, "student_grad", (sds((WIDTH, R), F32), sds((WIDTH, R), F32)), [VMEM] * 5
    )(normed, scaled, squared, pre, back)
    loss = (jnp.sum(back[TOK:]) / (TOK * D)).reshape(1)
    return loss, grad_up[None], grad_down[None]


def solution(mesh):
    in_specs = (P(), P("segment"), P("segment"), P("segment", "mp"), P("segment", None))
    out_specs = (P("segment"), P("segment", "mp", None), P("segment", "mp", None))
    return jax.shard_map(local, mesh=mesh, in_specs=in_specs, out_specs=out_specs, check_vma=False)
```

```python
import functools
import math

import jax
import jax.numpy as jnp
import numpy as np
from jax import lax
from jax.experimental import pallas as pl
from jax.experimental.pallas import tpu as pltpu
from jax.sharding import PartitionSpec as P

D = 16384
R = 128
TOK = 128
LAYERS = 8
SEG = 8
MP = 16
WIDTH = D // MP
PIECE = WIDTH // SEG
ROWS = TOK + 16
EPSILON = 1e-05
EMBED_KEY = 7919
BF = jnp.bfloat16
F32 = jnp.float32


def wrapped(value):
    value &= 0xFFFFFFFF
    return np.int32(value - (1 << 32) if value >> 31 else value)


MULT = wrapped(73244475)
MULT_SQ = wrapped(73244475 * 73244475)


def fold(bits):
    return jnp.bitwise_xor(bits, lax.shift_right_logical(bits, jnp.int32(16)))


def uniform_bits(mixed_bits):
    mixed_bits = fold(mixed_bits) * MULT
    mixed_bits = fold(mixed_bits) * MULT_SQ
    mixed_bits = fold(mixed_bits) * MULT
    return lax.shift_right_logical(fold(mixed_bits), jnp.int32(8))


def hashed(mixed_bits, magnitude):
    return uniform_bits(mixed_bits).astype(F32) * np.float32(magnitude * 2.0 / 16777216.0) - np.float32(magnitude)


def ternary(mixed_bits, magnitude):
    bits = uniform_bits(mixed_bits)
    return (lax.rem(bits, jnp.int32(3)) - jnp.int32(1)).astype(F32) * np.float32(magnitude)


def split_row(row):
    high = row.astype(BF).astype(F32)
    index = lax.broadcasted_iota(jnp.int32, (16, row.shape[1]), 0)
    tile = jnp.where(index == 0, high, jnp.where(index == 1, row - high, 0.0))
    return tile.astype(BF)


def joined_row(tile):
    return jnp.sum(tile.astype(F32), axis=0, keepdims=True)


SMEM = pl.BlockSpec(memory_space=pltpu.SMEM)
VMEM = pl.BlockSpec(memory_space=pltpu.VMEM)
HBM = pl.BlockSpec(memory_space=pltpu.HBM)


def call(body, name, out_shape, in_specs, flops=0, nbytes=0, limit=8 << 20, out_specs=None, scratch=(), aliases={}):
    single = not isinstance(out_shape, (tuple, list))
    return pl.pallas_call(
        body,
        out_shape=out_shape,
        in_specs=in_specs,
        out_specs=out_specs or (VMEM if single else tuple(VMEM for _ in out_shape)),
        scratch_shapes=scratch,
        input_output_aliases=aliases,
        name=name,
        cost_estimate=pl.CostEstimate(flops=flops, bytes_accessed=nbytes, transcendentals=0),
        compiler_params=pltpu.CompilerParams(vmem_limit_bytes=limit),
    )


def sds(shape, dtype):
    return jax.ShapeDtypeStruct(shape, dtype)


def gate(value, *others):
    return lax.optimization_barrier((value, *others))[0]


def pack_kernel(seed, gain, out):
    row = jnp.full((1, PIECE), seed[0], jnp.int32).astype(F32)
    for index in range(SEG):
        part = gain[:, index * PIECE : (index + 1) * PIECE].astype(F32)
        for target in range(SEG):
            out[target, index : index + 1, :] = part
    for target in range(SEG):
        out[target, SEG:, :] = jnp.broadcast_to(row, (SEG, PIECE))


def embed_kernel(place, token, stream_out, piece_out, tile_out):
    tokens = jnp.broadcast_to(token[...], (TOK, PIECE)) * 16411 + wrapped(EMBED_KEY * 1000003)
    tokens = tokens + lax.broadcasted_iota(jnp.int32, (TOK, PIECE), 1)
    squares = jnp.zeros((TOK, PIECE), F32)
    for index in range(SEG):
        part = hashed(tokens + (place[0] + index * PIECE), math.sqrt(3.0)).astype(BF)
        stream_out[:, index * PIECE : (index + 1) * PIECE] = part
        wide = part.astype(F32)
        squares = squares + wide * wide
    piece_out[...] = hashed(tokens + (place[0] + place[1] * PIECE), math.sqrt(3.0)).astype(BF)
    tile_out[...] = split_row(jnp.sum(jnp.transpose(squares), axis=0, keepdims=True))


def first_weight_kernel(place, out):
    chunk = 16
    shape = (chunk, MP * PIECE)
    row = lax.broadcasted_iota(jnp.int32, shape, 0)
    col = lax.broadcasted_iota(jnp.int32, shape, 1)
    base = row * 16411 + (col // PIECE) * WIDTH + col % PIECE + place[0]

    def step(index, carry):
        start = pl.multiple_of(index * chunk, chunk)
        out[pl.ds(start, chunk), :] = hashed(base + index * (chunk * 16411), math.sqrt(3.0 / D)).astype(BF)
        return carry

    lax.fori_loop(0, WIDTH // chunk, step, 0, unroll=2)


WIDE = 256
PARTS = WIDTH // WIDE


def weight_kernel(layer, place, *refs):
    out, slots, sems = refs[-3:]
    chunk, tall, depth = 64, 256, 4
    row = lax.broadcasted_iota(jnp.int32, (chunk, WIDTH), 0)
    col = lax.broadcasted_iota(jnp.int32, (chunk, WIDTH), 1)
    base = row * 16411 + col + place[layer]

    def copy(index, slot):
        start = pl.multiple_of(index * tall, tall)
        return pltpu.make_async_copy(slots.at[slot], out.at[layer - 1, :, pl.ds(start, tall), :], sems.at[slot])

    def fill(index, slot):
        def step(part, carry):
            first = (2 * index + part // 2) * (WIDTH * 16411) + (part % 2) * (chunk * 16411)
            made = hashed(base + first, math.sqrt(3.0 / D)).astype(BF)
            start = pl.multiple_of(part * chunk, chunk)
            for wide in range(PARTS):
                slots[slot, wide, pl.ds(start, chunk), :] = made[:, wide * WIDE : (wide + 1) * WIDE]
            return carry

        lax.fori_loop(0, tall // chunk, step, 0, unroll=2)
        copy(index, slot).start()

    def first_round(slot, carry):
        fill(slot, slot)
        return carry

    def second_round(slot, carry):
        copy(slot, slot).wait()
        fill(depth + slot, slot)
        return carry

    lax.fori_loop(0, depth, first_round, 0)
    lax.fori_loop(0, depth, second_round, 0)
    for slot in range(depth):
        copy(depth + slot, slot).wait()


WEIGHTS = MP * PIECE * WIDTH


def teacher_weight(layer, place, stored=None):
    cost = dict(flops=20 * WEIGHTS, nbytes=2 * WEIGHTS)
    if layer == 0:
        return call(first_weight_kernel, "first_weight", sds((WIDTH, MP * PIECE), BF), [SMEM], **cost)(place)
    return call(
        functools.partial(weight_kernel, layer),
        "weight",
        sds((LAYERS - 1, PARTS, MP * PIECE, WIDE), BF),
        [SMEM] + [HBM] * (layer > 1),
        out_specs=HBM,
        scratch=(pltpu.VMEM((4, PARTS, 256, WIDE), BF), pltpu.SemaphoreType.DMA((4,))),
        limit=40 << 20,
        aliases={1: 0} if layer > 1 else {},
        **cost,
    )(place, *([stored] if layer > 1 else []))


def first_contract_kernel(stream, tile, facts, weight, out):
    parts = []
    for index in range(SEG):
        part = stream[:, index * PIECE : (index + 1) * PIECE].astype(F32)
        parts.append((part * facts[0, index : index + 1, :]).astype(BF))
    scaled = jnp.concatenate(parts, axis=1)
    squares = tile[...]
    for index in range(MP // 2):
        part = jnp.dot(scaled, weight[:, index * 256 : (index + 1) * 256], preferred_element_type=F32)
        for half in range(2):
            out[2 * index + half, :TOK, :] = part[:, half * PIECE : (half + 1) * PIECE].astype(BF)
            out[2 * index + half, TOK:, :] = squares


def message(out, sems, held, stream, gain):
    wide = stream.astype(F32)
    scaled = (wide * gain).astype(BF)
    tile = split_row(jnp.sum(jnp.transpose(wide * wide), axis=0, keepdims=True))
    for index in range(4):
        held[index, :TOK, :] = scaled
        held[index, TOK:, :] = tile
    copies = [pltpu.make_async_copy(held, out.at[pl.ds(4 * index, 4)], sems.at[index]) for index in range(MP // 4)]
    for copy in copies:
        copy.start()
    for copy in copies:
        copy.wait()


def advance(layer, total, stream, gains, stream_out, mean_out, message_out, held, sems):
    squares = joined_row(total[TOK:])
    mean = jnp.transpose(jnp.broadcast_to(squares, (TOK, TOK))) * np.float32(1.0 / D)
    mean_out[...] = mean
    result = (stream[...].astype(F32) + total[:TOK] * lax.rsqrt(mean + EPSILON)).astype(BF)
    stream_out[...] = result
    message(message_out, sems, held, result, gains[layer + 1 : layer + 2, :])


def first_update_kernel(parts, stream, gains, stream_out, mean_out, message_out, held, sems):
    total = parts[0].astype(F32)
    for index in range(1, MP):
        total = total + parts[index].astype(F32)
    advance(0, total, stream, gains, stream_out, mean_out, message_out, held, sems)


def update_kernel(layer, own, part_a, part_b, part_c, stream, gains, stream_out, mean_out, message_out, held, sems):
    total = own[...]
    for part in (part_a, part_b, part_c):
        total = total + part[...].astype(F32)
    advance(layer, total, stream, gains, stream_out, mean_out, message_out, held, sems)


def contract_kernel(layer, place, gathered, weight, own_out, other_out, held, sems):
    half = MP * PIECE // 2
    copies = []
    for part in range(PARTS):
        for rows in range(2):
            where = (part, pl.ds(rows * half, half))
            copies.append(pltpu.make_async_copy(weight.at[(layer - 1, *where)], held.at[where], sems.at[part, rows]))
    for copy in copies:
        copy.start()
    scaled = jnp.concatenate([gathered[index, :TOK, :] for index in range(MP)], axis=1)
    squares = joined_row(gathered[0, TOK:, :])
    for index in range(1, MP):
        squares = squares + joined_row(gathered[index, TOK:, :])
    tile = split_row(squares)
    first = place[0] == 0
    for chunk in range(4):
        copies[2 * chunk].wait()
        copies[2 * chunk + 1].wait()
        part = jnp.dot(scaled, held[chunk], preferred_element_type=F32)
        left, right = part[:, :PIECE], part[:, PIECE:]
        own_out[chunk, :TOK, :] = jnp.where(first, left, right)
        other_out[chunk, :TOK, :] = jnp.where(first, right, left).astype(BF)
        own_out[chunk, TOK:, :] = tile.astype(F32)
        other_out[chunk, TOK:, :] = tile


def packed(both, out):
    out[:TOK, :] = both[:TOK].astype(BF)
    out[TOK:, :] = split_row(joined_row(both[TOK:]))


def pair_kernel(place, own, other, kept, send_a, send_b, send_c):
    here = place[0]
    kept[...] = own[here] + other[here].astype(F32)
    for shift, out in ((1, send_a), (2, send_b), (3, send_c)):
        chunk = lax.rem(here + shift, 4)
        packed(own[chunk] + other[chunk].astype(F32), out)


def last_pair_kernel(own, other, kept, send):
    for chunk in range(4):
        both = own[chunk] + other[chunk].astype(F32)
        kept[chunk] = both
        packed(both, send.at[chunk])


def last_update_kernel(place, kept, part_a, part_b, part_c, pieces, stream_out, mean_out):
    core = place[1]
    last = place[0] == SEG - 1
    for chunk in range(4):
        total = kept[chunk]
        for part in (part_a, part_b, part_c):
            total = total + part[chunk].astype(F32)
        if chunk == 0:
            squares = joined_row(total[TOK:])
            mean = jnp.transpose(jnp.broadcast_to(squares, (TOK, TOK))) * np.float32(1.0 / D)
            mean_out[...] = mean
            scale = lax.rsqrt(mean + EPSILON)
        before = pieces[2 * chunk + core].astype(F32)
        stream = jnp.where(last, before[0], before[1])
        stream_out[chunk] = (stream + total[:TOK] * scale).astype(BF)


def gather_kernel(place, *refs):
    streams, means = refs[:LAYERS], refs[LAYERS : 2 * LAYERS - 1]
    outs, mean_out, held = refs[2 * LAYERS - 1 : -2], refs[-2], refs[-1]
    for layer in range(LAYERS):
        held[layer] = streams[layer][...]
    held[LAYERS] = streams[LAYERS - 1][...]
    for partner in range(SEG):
        outs[partner][...] = held[pl.ds(jnp.bitwise_xor(place[0], partner), 2)]
    mean = means[0][...]
    for layer in range(1, LAYERS - 1):
        mean = jnp.where(place[0] == layer, means[layer][...], mean)
    mean_out[...] = mean


def partners(partner):
    return [(i, i ^ partner) for i in range(SEG)]


CORE = [(i, i ^ 1) for i in range(SEG)]


def along_x(shift):
    return [(i, (i + 2 * shift) % SEG) for i in range(SEG)]


def to_last(column):
    return [(2 * column + core, SEG - 2 + core) for core in range(2)]


def along_y(shift):
    return [(i, i // 4 * 4 + (i + shift) % 4) for i in range(MP)]


def along_z(shift):
    return [(i, (i + 4 * shift) % MP) for i in range(MP)]


def sum_mp(value):
    for along in (along_y, along_z):
        parts = [lax.ppermute(value, "mp", along(shift)) for shift in (1, 2, 3)]
        value = (value + parts[1]) + (parts[0] + parts[2])
    return value


def ternary_base(place):
    row = lax.broadcasted_iota(jnp.int32, (PIECE, R), 0)
    rank = lax.broadcasted_iota(jnp.int32, (PIECE, R), 1)
    return row * 16411 + rank + place


def student_up_kernel(place, gain, *refs):
    parts, pieces, pre_out = refs[:SEG], refs[SEG], refs[SEG + 1]
    for partner in range(SEG):
        pieces[jnp.bitwise_xor(place[0], partner)] = parts[partner][...]
    base = ternary_base(place[2])
    total = jnp.zeros((TOK, R), F32)
    for index in range(SEG):
        up_weight = ternary(base + index * PIECE * 16411, math.sqrt(1.5 / D)).astype(BF)
        scaled = (pieces[index, 0].astype(F32) * gain[:, index * PIECE : (index + 1) * PIECE].astype(F32)).astype(BF)
        total = total + jnp.dot(scaled, up_weight, preferred_element_type=F32)
    pre_out[...] = total


def student_error_kernel(place, pieces, own, other, pre, mean, last_mean, back_out, scaled_out, squared_out, pre_out):
    last = place[0] == SEG - 1
    first = place[1] == 0
    base = ternary_base(place[2] + R)
    scale = lax.rsqrt(jnp.where(last, last_mean[...], mean[...]) + EPSILON)
    rectified = jnp.maximum(pre[...] * scale, 0.0)
    pre_out[...] = rectified
    squared = (rectified * rectified).astype(BF)
    squared_out[...] = squared
    back = jnp.zeros((TOK, R), F32)
    squares = jnp.zeros((TOK, PIECE), F32)
    for index in range(SEG):
        down_weight = ternary(base + index * PIECE * 16411, math.sqrt(1.5 / R)).astype(BF)
        student = lax.dot_general(squared, down_weight, (((1,), (1,)), ((), ())), preferred_element_type=F32)
        mine, theirs = own[index // 2].astype(F32), other[index // 2].astype(F32)
        final = jnp.where(first, mine, theirs) if index % 2 == 0 else jnp.where(first, theirs, mine)
        target = jnp.where(last, final, pieces[index, 1].astype(F32))
        error = pieces[index, 0].astype(F32) + student - target
        squares = squares + error * error
        scaled = (error * np.float32(1.0 / TOK)).astype(BF)
        scaled_out[:, index * PIECE : (index + 1) * PIECE] = scaled
        back = back + jnp.dot(scaled, down_weight, preferred_element_type=F32)
    back_out[:TOK, :] = back
    back_out[TOK:, :] = jnp.sum(squares.reshape(TOK // 8, 8, PIECE), axis=0)


OVER_TOKENS = (((0,), (0,)), ((), ()))


def student_down_kernel(place, pieces, gain, mean, last_mean, scaled, squared, normed_out, down_out):
    scale = lax.rsqrt(jnp.where(place[0] == SEG - 1, last_mean[...], mean[...]) + EPSILON)
    for index in range(SEG):
        columns = slice(index * PIECE, (index + 1) * PIECE)
        normed = pieces[index, 0].astype(F32) * scale * gain[:, columns].astype(F32)
        normed_out[:, columns] = normed.astype(BF)
    down_out[...] = lax.dot_general(scaled[...], squared[...], OVER_TOKENS, preferred_element_type=F32)


def student_grad_kernel(normed, rectified, back, up_out, loss_out):
    back_pre = (back[:TOK, :] * 2.0 * rectified[...]).astype(BF)
    up_out[...] = lax.dot_general(normed[...], back_pre, OVER_TOKENS, preferred_element_type=F32)
    total = jnp.sum(jnp.sum(back[TOK:, :], axis=0, keepdims=True), axis=1, keepdims=True)
    loss_out[...] = total * np.float32(1.0 / (TOK * D))


def local(token_ids, teacher_seeds, student_seeds, teacher_gain, student_gain):
    block = lax.axis_index("mp")
    segment = lax.axis_index("segment")
    core = lax.rem(segment, 2)
    column = segment // 2
    piece_shape = sds((TOK, PIECE), BF)
    mean_shape = sds((TOK, TOK), F32)
    message_shape = sds((MP, ROWS, PIECE), BF)

    facts = call(pack_kernel, "pack", sds((SEG, 2 * SEG, PIECE), F32), [SMEM, VMEM])(teacher_seeds, teacher_gain)
    facts = lax.all_to_all(facts, "segment", split_axis=0, concat_axis=0, tiled=True)
    embedded, stream, tile = call(
        embed_kernel, "embed", (sds((TOK, WIDTH), BF), piece_shape, sds((16, TOK), BF)), [SMEM, VMEM]
    )(jnp.stack([block * WIDTH, segment]), token_ids.reshape(TOK, 1))
    here = segment * PIECE * 16411 + block * WIDTH
    first_here = block * (WIDTH * 16411) + segment * PIECE
    at_start = jnp.arange(LAYERS, dtype=jnp.int32) == 0
    places = facts[:, SEG, 0].astype(jnp.int32) * 1000003 + jnp.where(at_start, first_here, here)
    gains = lax.dynamic_index_in_dim(facts, segment, 1, False)

    weight = teacher_weight(0, places)
    outgoing = call(
        first_contract_kernel, "first_contract", message_shape, [VMEM] * 4, flops=2 * TOK * WEIGHTS, nbytes=2 * WEIGHTS
    )(embedded, tile, facts, weight)
    parts = lax.all_to_all(outgoing, "mp", split_axis=0, concat_axis=0, tiled=True)
    weight = teacher_weight(1, gate(places, outgoing))
    parts, weight = lax.optimization_barrier((parts, weight))
    advance_out = dict(
        out_shape=(piece_shape, mean_shape, message_shape),
        out_specs=(VMEM, VMEM, HBM),
        scratch=(pltpu.VMEM((4, ROWS, PIECE), BF), pltpu.SemaphoreType.DMA((MP // 4,))),
    )
    stream_new, mean, outgoing = call(first_update_kernel, "first_update", in_specs=[VMEM] * 3, **advance_out)(
        parts, stream, gains
    )
    streams, means = [stream, stream_new], [mean]
    for layer in range(1, LAYERS):
        gathered = lax.all_to_all(outgoing, "mp", split_axis=0, concat_axis=0, tiled=True)
        if layer + 1 < LAYERS:
            weight = teacher_weight(layer + 1, gate(places, outgoing), weight)
            gathered, weight = lax.optimization_barrier((gathered, weight))
        else:
            place = jnp.stack([segment, core, student_seeds[0] * 1000003 + block * (WIDTH * 16411)])
            *pairs, mean = call(
                gather_kernel,
                "gather",
                tuple(sds((2, TOK, PIECE), BF) for _ in range(SEG)) + (mean_shape,),
                [SMEM] + [VMEM] * (2 * LAYERS - 1),
                scratch=(pltpu.VMEM((LAYERS + 1, TOK, PIECE), BF),),
            )(place, *streams, *means)
            pairs[1:] = [lax.ppermute(pairs[partner], "segment", partners(partner)) for partner in range(1, SEG)]
            gathered = gate(gathered, *pairs)
        own, other = call(
            functools.partial(contract_kernel, layer),
            "contract",
            (sds((4, ROWS, PIECE), F32), sds((4, ROWS, PIECE), BF)),
            [SMEM, VMEM, HBM],
            flops=2 * TOK * WEIGHTS,
            nbytes=2 * WEIGHTS,
            limit=40 << 20,
            scratch=(pltpu.VMEM((PARTS, MP * PIECE, WIDE), BF), pltpu.SemaphoreType.DMA((PARTS, 2))),
        )(core.reshape(1), gathered, weight)
        other = lax.ppermute(other, "segment", CORE)
        if layer + 1 == LAYERS:
            break
        kept, *sends = call(
            pair_kernel,
            "pair",
            (sds((ROWS, PIECE), F32),) + tuple(sds((ROWS, PIECE), BF) for _ in range(3)),
            [SMEM, VMEM, VMEM],
        )(column.reshape(1), own, other)
        parts = [lax.ppermute(send, "segment", along_x(shift)) for shift, send in zip((1, 2, 3), sends)]
        stream, mean, outgoing = call(
            functools.partial(update_kernel, layer), "update", in_specs=[VMEM] * 6, **advance_out
        )(kept, *parts, streams[-1], gains)
        streams.append(stream)
        means.append(mean)

    kept, send = call(
        last_pair_kernel, "last_pair", (sds((4, ROWS, PIECE), F32), sds((4, ROWS, PIECE), BF)), [VMEM] * 2
    )(own, other)
    parts = [lax.ppermute(send, "segment", to_last(source)) for source in range(3)]
    student_columns = lax.dynamic_slice_in_dim(student_gain, block * WIDTH, WIDTH, 1)
    pieces, pre = call(
        student_up_kernel,
        "student_up",
        (sds((SEG, 2, TOK, PIECE), BF), sds((TOK, R), F32)),
        [SMEM] + [VMEM] * (SEG + 1),
    )(place, student_columns, gate(pairs[0], send), *pairs[1:])
    pre = sum_mp(pre)
    last_own, last_mean = call(
        last_update_kernel, "last_update", (sds((4, TOK, PIECE), BF), mean_shape), [SMEM] + [VMEM] * 5
    )(place, kept, *parts, pieces)
    last_other = lax.ppermute(last_own, "segment", CORE)

    back, scaled, squared, rectified = call(
        student_error_kernel,
        "student_error",
        (sds((TOK + 8, R), F32), sds((TOK, WIDTH), BF), sds((TOK, R), BF), sds((TOK, R), F32)),
        [SMEM] + [VMEM] * 6,
    )(place, pieces, last_own, last_other, pre, mean, last_mean)
    normed, grad_down = call(
        student_down_kernel, "student_down", (sds((TOK, WIDTH), BF), sds((WIDTH, R), F32)), [SMEM] + [VMEM] * 6
    )(place, pieces, student_columns, mean, last_mean, scaled, squared)
    back = sum_mp(back)
    grad_up, loss = call(
        student_grad_kernel, "student_grad", (sds((WIDTH, R), F32), sds((1, 1), F32)), [VMEM] * 3
    )(normed, rectified, back)
    return loss.reshape(1), grad_up[None], grad_down[None]


def solution(mesh):
    in_specs = (P(), P("segment"), P("segment"), P("segment", "mp"), P("segment", None))
    out_specs = (P("segment"), P("segment", "mp", None), P("segment", "mp", None))
    return jax.shard_map(local, mesh=mesh, in_specs=in_specs, out_specs=out_specs, check_vma=False)
```

```python
import functools
import math

import jax
import jax.numpy as jnp
import numpy as np
from jax import lax
from jax.experimental import pallas as pl
from jax.experimental.pallas import tpu as pltpu
from jax.sharding import PartitionSpec as P

D = 16384
R = 128
TOK = 128
LAYERS = 8
SEG = 8
MP = 16
WIDTH = D // MP
PIECE = WIDTH // SEG
STATE = 4 * TOK
GATHER = STATE + 16
SUM = STATE + TOK + 16
STEP_Q, STEP_P, STEP_R, STEP_C = 4096, 1024, 256, 128
EPSILON = 1e-05
EMBED_KEY = 7919
BF = jnp.bfloat16
F32 = jnp.float32


def wrapped(value):
    value &= 0xFFFFFFFF
    return np.int32(value - (1 << 32) if value >> 31 else value)


MULT = wrapped(73244475)
MULT_SQ = wrapped(73244475 * 73244475)


def fold(bits):
    return jnp.bitwise_xor(bits, lax.shift_right_logical(bits, jnp.int32(16)))


def uniform_bits(mixed_bits):
    mixed_bits = fold(mixed_bits) * MULT
    mixed_bits = fold(mixed_bits) * MULT_SQ
    mixed_bits = fold(mixed_bits) * MULT
    return lax.shift_right_logical(fold(mixed_bits), jnp.int32(8))


def hashed(mixed_bits, magnitude):
    return uniform_bits(mixed_bits).astype(F32) * np.float32(magnitude * 2.0 / 16777216.0) - np.float32(magnitude)


def ternary(mixed_bits, magnitude):
    bits = uniform_bits(mixed_bits)
    return (lax.rem(bits, jnp.int32(3)) - jnp.int32(1)).astype(F32) * np.float32(magnitude)


def split_row(row):
    high = row.astype(BF).astype(F32)
    index = lax.broadcasted_iota(jnp.int32, (16, row.shape[1]), 0)
    tile = jnp.where(index == 0, high, jnp.where(index == 1, row - high, 0.0))
    return tile.astype(BF)


def joined_row(tile):
    return jnp.sum(tile.astype(F32), axis=0, keepdims=True)


SMEM = pl.BlockSpec(memory_space=pltpu.SMEM)
VMEM = pl.BlockSpec(memory_space=pltpu.VMEM)
HBM = pl.BlockSpec(memory_space=pltpu.HBM)


def call(body, name, out_shape, in_specs, flops=0, nbytes=0, limit=8 << 20, out_specs=None, scratch=(), aliases={}):
    single = not isinstance(out_shape, (tuple, list))
    return pl.pallas_call(
        body,
        out_shape=out_shape,
        in_specs=in_specs,
        out_specs=out_specs or (VMEM if single else tuple(VMEM for _ in out_shape)),
        scratch_shapes=scratch,
        input_output_aliases=aliases,
        name=name,
        cost_estimate=pl.CostEstimate(flops=flops, bytes_accessed=nbytes, transcendentals=0),
        compiler_params=pltpu.CompilerParams(vmem_limit_bytes=limit),
    )


def sds(shape, dtype):
    return jax.ShapeDtypeStruct(shape, dtype)


def gate(value, *others):
    return lax.optimization_barrier((value, *others))[0]


def pack_kernel(seed, gain, out):
    row = jnp.full((1, PIECE), seed[0], jnp.int32).astype(F32)
    for index in range(SEG):
        part = gain[:, index * PIECE : (index + 1) * PIECE].astype(F32)
        for target in range(SEG):
            out[target, index : index + 1, :] = part
    for target in range(SEG):
        out[target, SEG:, :] = jnp.broadcast_to(row, (SEG, PIECE))


def facts_kernel(place, student_seed, facts, along_z_out, along_y_out, even_out, place_out, student_out):
    core, column, row, plane = place[1], place[2], place[3], place[4]
    for digit in range(4):
        along_z_out[digit] = facts[0, pl.ds(2 * digit + core, 1), :]
        along_y_out[digit] = facts[2 * digit + 1, pl.ds(2 * column + core, 1), :]
        for pair in range(4):
            even_out[pair, digit] = facts[2 * pair, pl.ds(2 * digit + core, 1), :]
    even = (row * STEP_P + core * STEP_C) * 16411 + plane * STEP_Q + column * STEP_R
    odd = (column * STEP_R + core * STEP_C) * 16411 + plane * STEP_Q + row * STEP_P
    for layer in range(LAYERS):
        seed = facts[layer, SEG : SEG + 1, :].astype(jnp.int32)
        place_out[layer : layer + 1, :] = seed * 1000003 + (even if layer % 2 == 0 else odd)
    block = plane * 4 + row
    student_out[...] = jnp.full((SEG, PIECE), student_seed[0] * 1000003 + block * (WIDTH * 16411), jnp.int32)


def odd_gain_kernel(row, *refs):
    parts, out = refs[:4], refs[4]
    for partner, part in zip(PARTNERS, parts):
        for pair in range(4):
            out[pair, jnp.bitwise_xor(row[0], partner)] = part[pair]


def squares_tile(squares):
    return split_row(jnp.sum(jnp.transpose(squares), axis=0, keepdims=True))


def embed_kernel(place, token, out, tile_out):
    tokens = jnp.broadcast_to(token[...], (TOK, PIECE)) * 16411 + wrapped(EMBED_KEY * 1000003)
    tokens = tokens + lax.broadcasted_iota(jnp.int32, (TOK, PIECE), 1)
    tokens = tokens + (place[1] * STEP_C + place[3] * STEP_P)
    squares = jnp.zeros((TOK, PIECE), F32)
    for slot, partner in enumerate(PARTNERS):
        for digit in range(4):
            first = jnp.bitwise_xor(place[4], partner) * STEP_Q + digit * STEP_R
            part = hashed(tokens + first, math.sqrt(3.0)).astype(BF)
            out[slot, digit * TOK : (digit + 1) * TOK, :] = part
            wide = part.astype(F32)
            squares = squares + wide * wide
    tile_out[...] = squares_tile(squares)


def first_scale_kernel(embedded, tile, *refs):
    gains, outs = refs[:4], refs[4:]
    for partner in range(4):
        for digit in range(4):
            rows = slice(digit * TOK, (digit + 1) * TOK)
            outs[partner][rows, :] = (embedded[partner, rows, :].astype(F32) * gains[partner][digit]).astype(BF)
        outs[partner][STATE:, :] = tile[...] if partner == 0 else jnp.zeros((16, TOK), BF)


def weight_kernel(layer, plane, place, out):
    chunk = 64
    row_step, col_step = (STEP_R, STEP_P) if layer % 2 == 0 else (STEP_P, STEP_R)
    row = lax.broadcasted_iota(jnp.int32, (chunk, WIDTH), 0)
    col = lax.broadcasted_iota(jnp.int32, (chunk, WIDTH), 1)
    col = (col // 512) * STEP_C + (col // PIECE % 4) * col_step + col % PIECE
    base = row * 16411 + col + jnp.concatenate([place[layer : layer + 1, :]] * (WIDTH // PIECE), axis=1)

    def step(index, carry):
        piece = index // 2
        slot = piece // 4
        partner = jnp.where(slot == 0, 0, jnp.where(slot == 1, PARTNERS[1], slot - 1))
        first = jnp.bitwise_xor(plane[0], partner) * (STEP_Q * 16411) + (piece % 4) * (row_step * 16411) + (index % 2) * (chunk * 16411)
        start = pl.multiple_of(index * chunk, chunk)
        out[pl.ds(start, chunk), :] = hashed(base + first, math.sqrt(3.0 / D)).astype(BF)
        return carry

    lax.fori_loop(0, 2048 // chunk, step, 0, unroll=2)


WEIGHTS = 2048 * WIDTH


def teacher_weight(layer, plane, place):
    body = functools.partial(weight_kernel, layer)
    return call(body, "weight", sds((2048, WIDTH), BF), [SMEM, VMEM], flops=20 * WEIGHTS, nbytes=2 * WEIGHTS)(
        plane, place
    )


def contract_kernel(core, *refs):
    parts, (weight, own_out, other_out) = refs[:4], refs[4:]
    scaled = [part[digit * TOK : (digit + 1) * TOK, :] for part in parts for digit in range(4)]
    scaled = jnp.concatenate(scaled, axis=1)
    squares = joined_row(parts[0][STATE:, :])
    for part in parts[1:]:
        squares = squares + joined_row(part[STATE:, :])
    tile = split_row(squares)
    own_out[STATE:, :] = tile.astype(F32)
    other_out[STATE:, :] = tile
    first = core[0] == 0
    for pair in range(2):
        low = jnp.dot(scaled, weight[:, pair * 256 : (pair + 1) * 256], preferred_element_type=F32)
        high = jnp.dot(scaled, weight[:, 512 + pair * 256 : 512 + (pair + 1) * 256], preferred_element_type=F32)
        own, other = jnp.where(first, low, high), jnp.where(first, high, low).astype(BF)
        for half in range(2):
            rows = slice((2 * pair + half) * TOK, (2 * pair + half + 1) * TOK)
            columns = slice(half * PIECE, (half + 1) * PIECE)
            own_out[rows, :] = own[:, columns]
            other_out[rows, :] = other[:, columns]


def pair_kernel(digit, own, other, stream, out):
    total = own[...] + other[...].astype(F32)
    out[:STATE, :] = total[:STATE].astype(BF)
    start = pl.multiple_of(digit[0] * TOK, TOK)
    out[STATE : STATE + TOK, :] = stream[pl.ds(start, TOK), :]
    out[STATE + TOK :, :] = split_row(joined_row(total[STATE:]))


def update_kernel(pair, digit, part_a, part_b, part_c, part_d, gains, stream_out, mean_out, message_out):
    parts = (part_a, part_b, part_c, part_d)

    def total(rows):
        wide = [part[rows, :].astype(F32) for part in parts]
        return (wide[0] + wide[2]) + (wide[1] + wide[3])

    squares = joined_row(total(slice(STATE + TOK, SUM)))
    mean = jnp.transpose(jnp.broadcast_to(squares, (TOK, TOK))) * np.float32(1.0 / D)
    mean_out[...] = mean
    scale = lax.rsqrt(mean + EPSILON)
    for partner, part in zip(PARTNERS, parts):
        start = pl.multiple_of(jnp.bitwise_xor(digit[0], partner) * TOK, TOK)
        stream_out[pl.ds(start, TOK), :] = part[STATE : STATE + TOK, :]
    squares = jnp.zeros((TOK, PIECE), F32)
    for index in range(4):
        rows = slice(index * TOK, (index + 1) * TOK)
        result = (stream_out[rows, :].astype(F32) + total(rows) * scale).astype(BF)
        stream_out[rows, :] = result
        wide = result.astype(F32)
        squares = squares + wide * wide
        if pair is not None:
            message_out[rows, :] = (wide * gains[pair, index]).astype(BF)
    if pair is not None:
        message_out[STATE:, :] = squares_tile(squares)


def odd_kernel(column, row, *refs):
    streams, outs, held = refs[:4], refs[4:8], refs[8]
    start = pl.multiple_of(row[0] * TOK, TOK)
    for index in range(4):
        held[index] = streams[index][pl.ds(start, TOK), :]
    for partner in range(4):
        outs[partner][...] = held[jnp.bitwise_xor(column[0], partner)]


def first_swap_kernel(segment, core, column, *refs):
    odd_parts, even, means = refs[:4], refs[4:8], refs[8:15]
    odd_out, here_out, send_out, later_out, mean_out = refs[15:20]
    held = refs[20]
    first = core[0] == 0
    for partner, part in zip(PARTNERS, odd_parts):
        start = pl.multiple_of(jnp.bitwise_xor(column[0], partner) * TOK, TOK)
        odd_out[pl.ds(start, TOK), :] = part[...]
    for index in range(4):
        held[index] = even[index][...]
    held[4] = even[3][...]
    now = held[column[0]].astype(F32)
    odd = odd_out[...].astype(F32)
    here_out[...] = jnp.where(first, now, odd).astype(BF)
    send_out[...] = jnp.where(first, odd, now).astype(BF)
    later_out[...] = held[column[0] + 1]
    mean = means[0][...]
    for layer in range(1, LAYERS - 1):
        mean = jnp.where(segment[0] == layer, means[layer][...], mean)
    mean_out[...] = mean


def second_swap_kernel(core, column, odd, later, last, here_out, send_out):
    first = core[0] == 0
    even = jnp.where(column[0] == 3, last[...].astype(F32), later[...].astype(F32))
    odd = odd[...].astype(F32)
    here_out[...] = jnp.where(first, odd, even).astype(BF)
    send_out[...] = jnp.where(first, even, odd).astype(BF)


CORE = [(i, i ^ 1) for i in range(SEG)]
ALONG = {
    "x": ("segment", 2),
    "y": ("mp", 1),
    "z": ("mp", 4),
}


PARTNERS = (0, 3, 1, 2)


def exchange(values, physical):
    axis, step = ALONG[physical]
    size = SEG if axis == "segment" else MP
    values = values if isinstance(values, (list, tuple)) else [values] * 4
    return [values[0]] + [
        lax.ppermute(values[k], axis, [(i, i ^ (k * step)) for i in range(size)]) for k in PARTNERS[1:]
    ]


def sum_mp(value):
    for physical in ("y", "z"):
        own, third, first, second = exchange(value, physical)
        value = (own + first) + (second + third)
    return value


def ternary_base(place):
    row = lax.broadcasted_iota(jnp.int32, (PIECE, R), 0)
    rank = lax.broadcasted_iota(jnp.int32, (PIECE, R), 1)
    return row * 16411 + rank + place[0:1, :]


def piece_of(core, index, here, there):
    first = core[0] == 0
    rows = slice(index // 2 * TOK, (index // 2 + 1) * TOK)
    here, there = here[rows, :].astype(F32), there[rows, :].astype(F32)
    return jnp.where(first, here, there) if index % 2 == 0 else jnp.where(first, there, here)


def student_up_kernel(core, place, here, there, gain, pre_out):
    base = ternary_base(place)
    total = jnp.zeros((TOK, R), F32)
    for index in range(SEG):
        up_weight = ternary(base + index * PIECE * 16411, math.sqrt(1.5 / D)).astype(BF)
        gains = gain[:, index * PIECE : (index + 1) * PIECE].astype(F32)
        scaled = (piece_of(core, index, here, there) * gains).astype(BF)
        total = total + jnp.dot(scaled, up_weight, preferred_element_type=F32)
    pre_out[...] = total


def student_error_kernel(
    segment, core, place, here, there, target_here, target_there, pre, mean, last_mean, back_out, scaled_out, squared_out, pre_out
):
    base = ternary_base(place) + R
    scale = lax.rsqrt(jnp.where(segment[0] == SEG - 1, last_mean[...], mean[...]) + EPSILON)
    rectified = jnp.maximum(pre[...] * scale, 0.0)
    pre_out[...] = rectified
    squared = (rectified * rectified).astype(BF)
    squared_out[...] = squared
    back = jnp.zeros((TOK, R), F32)
    squares = jnp.zeros((TOK, PIECE), F32)
    for index in range(SEG):
        down_weight = ternary(base + index * PIECE * 16411, math.sqrt(1.5 / R)).astype(BF)
        student = lax.dot_general(squared, down_weight, (((1,), (1,)), ((), ())), preferred_element_type=F32)
        target = piece_of(core, index, target_here, target_there)
        error = piece_of(core, index, here, there) + student - target
        squares = squares + error * error
        scaled = (error * np.float32(1.0 / TOK)).astype(BF)
        scaled_out[:, index * PIECE : (index + 1) * PIECE] = scaled
        back = back + jnp.dot(scaled, down_weight, preferred_element_type=F32)
    back_out[:TOK, :] = back
    back_out[TOK:, :] = jnp.sum(squares.reshape(TOK // 8, 8, PIECE), axis=0)


OVER_TOKENS = (((0,), (0,)), ((), ()))


def student_down_kernel(segment, core, here, there, gain, mean, last_mean, scaled, squared, normed_out, down_out):
    scale = lax.rsqrt(jnp.where(segment[0] == SEG - 1, last_mean[...], mean[...]) + EPSILON)
    for index in range(SEG):
        columns = slice(index * PIECE, (index + 1) * PIECE)
        normed = piece_of(core, index, here, there) * scale * gain[:, columns].astype(F32)
        normed_out[:, columns] = normed.astype(BF)
    down_out[...] = lax.dot_general(scaled[...], squared[...], OVER_TOKENS, preferred_element_type=F32)


def student_grad_kernel(normed, rectified, back, up_out, loss_out):
    back_pre = (back[:TOK, :] * 2.0 * rectified[...]).astype(BF)
    up_out[...] = lax.dot_general(normed[...], back_pre, OVER_TOKENS, preferred_element_type=F32)
    total = jnp.sum(jnp.sum(back[TOK:, :], axis=0, keepdims=True), axis=1, keepdims=True)
    loss_out[...] = total * np.float32(1.0 / (TOK * D))


def local(token_ids, teacher_seeds, student_seeds, teacher_gain, student_gain):
    block = lax.axis_index("mp")
    segment = lax.axis_index("segment")
    core, column = lax.rem(segment, 2), segment // 2
    row, plane = lax.rem(block, 4), block // 4
    place = jnp.stack([segment, core, column, row, plane])
    segment, core, column, row, plane = (part.reshape(1) for part in (segment, core, column, row, plane))
    mean_shape = sds((TOK, TOK), F32)
    state_shape = sds((STATE, PIECE), BF)
    gain_shape = sds((4, 1, PIECE), F32)

    facts = call(pack_kernel, "pack", sds((SEG, 2 * SEG, PIECE), F32), [SMEM, VMEM])(teacher_seeds, teacher_gain)
    facts = lax.all_to_all(facts, "segment", split_axis=0, concat_axis=0, tiled=True)
    embedded, tile = call(
        embed_kernel, "embed", (sds((4, STATE, PIECE), BF), sds((16, TOK), BF)), [SMEM, VMEM]
    )(place, token_ids.reshape(TOK, 1))
    first_gain, odd_gain, even_gains, places, student_place = call(
        facts_kernel,
        "facts",
        (gain_shape, gain_shape, sds((4, 4, 1, PIECE), F32)) + (sds((LAYERS, PIECE), jnp.int32),) * 2,
        [SMEM, SMEM, VMEM],
    )(place, student_seeds, facts)
    first_gains = exchange(first_gain, "z")
    weight = teacher_weight(0, plane, places)
    parts = call(
        first_scale_kernel, "first_scale", tuple(sds((GATHER, PIECE), BF) for _ in range(4)), [VMEM] * 6
    )(embedded, tile, *first_gains)
    odd_gains = call(odd_gain_kernel, "odd_gain", sds((4, 4, 1, PIECE), F32), [SMEM] + [VMEM] * 4)(
        row, *exchange(gate(odd_gain, weight), "y")
    )

    streams, means = [embedded[0]], []
    for layer in range(LAYERS):
        if layer:
            weight = teacher_weight(layer, plane, gate(places, message))
            parts = exchange(message, "z")
        own, other = call(
            contract_kernel,
            "contract",
            (sds((GATHER, PIECE), F32), sds((GATHER, PIECE), BF)),
            [SMEM] + [VMEM] * 5,
            flops=2 * TOK * WEIGHTS,
            nbytes=2 * WEIGHTS,
        )(core, *parts, weight)
        other = lax.ppermute(other, "segment", CORE)
        even = layer % 2 == 0
        summed = call(
            pair_kernel, "pair", sds((SUM, PIECE), BF), [SMEM] + [VMEM] * 3
        )(column if even else row, own, other, streams[-1])
        parts = exchange(summed, "y" if even else "x")
        pair = None if layer + 1 == LAYERS else (layer + 1) // 2
        stream, mean, message = call(
            functools.partial(update_kernel, pair),
            "update",
            (state_shape, mean_shape, sds((GATHER, PIECE), BF)),
            [SMEM] + [VMEM] * 5,
        )(row if even else column, *parts, odd_gains if even else even_gains)
        streams.append(stream)
        means.append(mean)

    odd = call(
        odd_kernel,
        "odd",
        tuple(sds((TOK, PIECE), BF) for _ in range(4)),
        [SMEM] * 2 + [VMEM] * 4,
        scratch=(pltpu.VMEM((4, TOK, PIECE), BF),),
    )(column, row, *streams[1::2])
    odd = exchange(odd, "x")
    odd_half, here, send, later, mean = call(
        first_swap_kernel,
        "first_swap",
        (state_shape,) * 4 + (mean_shape,),
        [SMEM] * 3 + [VMEM] * 15,
        scratch=(pltpu.VMEM((5, STATE, PIECE), BF),),
    )(segment, core, column, *odd, *streams[0:8:2], *means[:7])
    there = lax.ppermute(send, "segment", CORE)
    student_columns = lax.dynamic_slice_in_dim(student_gain, block * WIDTH, WIDTH, 1)
    pre = call(student_up_kernel, "student_up", sds((TOK, R), F32), [SMEM] + [VMEM] * 4)(
        core, student_place, here, there, student_columns
    )
    pre = sum_mp(pre)

    target_here, send = call(second_swap_kernel, "second_swap", (state_shape,) * 2, [SMEM] * 2 + [VMEM] * 3)(
        core, column, odd_half, later, streams[LAYERS]
    )
    target_there = lax.ppermute(send, "segment", CORE)
    back, scaled, squared, rectified = call(
        student_error_kernel,
        "student_error",
        (sds((TOK + 8, R), F32), sds((TOK, WIDTH), BF), sds((TOK, R), BF), sds((TOK, R), F32)),
        [SMEM] * 2 + [VMEM] * 8,
    )(segment, core, student_place, here, there, target_here, target_there, pre, mean, means[LAYERS - 1])
    normed, grad_down = call(
        student_down_kernel, "student_down", (sds((TOK, WIDTH), BF), sds((WIDTH, R), F32)), [SMEM] * 2 + [VMEM] * 7
    )(segment, core, here, there, student_columns, mean, means[LAYERS - 1], scaled, squared)
    back = sum_mp(back)
    grad_up, loss = call(
        student_grad_kernel, "student_grad", (sds((WIDTH, R), F32), sds((1, 1), F32)), [VMEM] * 3
    )(normed, rectified, back)
    return loss.reshape(1), grad_up[None], grad_down[None]


def solution(mesh):
    in_specs = (P(), P("segment"), P("segment"), P("segment", "mp"), P("segment", None))
    out_specs = (P("segment"), P("segment", "mp", None), P("segment", "mp", None))
    return jax.shard_map(local, mesh=mesh, in_specs=in_specs, out_specs=out_specs, check_vma=False)
```

```python
import functools
import math

import jax
import jax.numpy as jnp
import numpy as np
from jax import lax
from jax.experimental import pallas as pl
from jax.experimental.pallas import tpu as pltpu
from jax.sharding import PartitionSpec as P

D = 16384
R = 128
TOK = 128
LAYERS = 8
SEG = 8
MP = 16
WIDTH = D // MP
PIECE = WIDTH // SEG
STATE = 4 * TOK
GATHER = STATE + 16
SUM = STATE + TOK + 16
FACTS = 48
STEP_Q, STEP_P, STEP_R, STEP_C = 4096, 1024, 256, 128
EPSILON = 1e-05
EMBED_KEY = 7919
BF = jnp.bfloat16
F32 = jnp.float32


def wrapped(value):
    value &= 0xFFFFFFFF
    return np.int32(value - (1 << 32) if value >> 31 else value)


MULT = wrapped(73244475)
MULT_SQ = wrapped(73244475 * 73244475)


def fold(bits):
    return jnp.bitwise_xor(bits, lax.shift_right_logical(bits, jnp.int32(16)))


def uniform_bits(mixed_bits):
    mixed_bits = fold(mixed_bits) * MULT
    mixed_bits = fold(mixed_bits) * MULT_SQ
    mixed_bits = fold(mixed_bits) * MULT
    return lax.shift_right_logical(fold(mixed_bits), jnp.int32(8))


def hashed(mixed_bits, magnitude):
    return uniform_bits(mixed_bits).astype(F32) * np.float32(magnitude * 2.0 / 16777216.0) - np.float32(magnitude)


def ternary(mixed_bits, magnitude):
    bits = uniform_bits(mixed_bits)
    return (lax.rem(bits, jnp.int32(3)) - jnp.int32(1)).astype(F32) * np.float32(magnitude)


def split_row(row):
    high = row.astype(BF).astype(F32)
    index = lax.broadcasted_iota(jnp.int32, (16, row.shape[1]), 0)
    tile = jnp.where(index == 0, high, jnp.where(index == 1, row - high, 0.0))
    return tile.astype(BF)


def joined_row(tile):
    return jnp.sum(tile.astype(F32), axis=0, keepdims=True)


SMEM = pl.BlockSpec(memory_space=pltpu.SMEM)
VMEM = pl.BlockSpec(memory_space=pltpu.VMEM)
HBM = pl.BlockSpec(memory_space=pltpu.HBM)


def call(body, name, out_shape, in_specs, flops=0, nbytes=0, limit=8 << 20, out_specs=None, scratch=(), aliases={}):
    single = not isinstance(out_shape, (tuple, list))
    return pl.pallas_call(
        body,
        out_shape=out_shape,
        in_specs=in_specs,
        out_specs=out_specs or (VMEM if single else tuple(VMEM for _ in out_shape)),
        scratch_shapes=scratch,
        input_output_aliases=aliases,
        name=name,
        cost_estimate=pl.CostEstimate(flops=flops, bytes_accessed=nbytes, transcendentals=0),
        compiler_params=pltpu.CompilerParams(vmem_limit_bytes=limit),
    )


def sds(shape, dtype):
    return jax.ShapeDtypeStruct(shape, dtype)


def gate(value, *others):
    return lax.optimization_barrier((value, *others))[0]


def pack_kernel(seed, student_seed, plane, gain, student_gain, out):
    rows = [gain[:, index * PIECE : (index + 1) * PIECE] for index in range(SEG)]
    for value in (seed[0], student_seed[0]):
        for shift in (16, 8, 0):
            byte = jnp.bitwise_and(lax.shift_right_logical(value, jnp.int32(shift)), jnp.int32(255))
            rows.append(jnp.full((1, PIECE), byte, jnp.int32).astype(F32).astype(BF))
    rows += [jnp.zeros((1, PIECE), BF)] * 2
    start = plane[0] * STEP_Q
    for index in range(4 * SEG):
        rows.append(student_gain[:, pl.ds(pl.multiple_of(start + index * PIECE, PIECE), PIECE)])
    for first in range(0, FACTS, 16):
        out[first : first + 16, :] = jnp.concatenate([row.astype(F32) for row in rows[first : first + 16]], axis=0).astype(BF)


def chip_kernel(core, own, other, out):
    out[core[0]] = own[...]
    out[1 - core[0]] = other[...]


def facts_kernel(place, student_seed, *refs):
    parts, (along_z_out, along_y_out, even_out, place_out, student_out) = refs[:4], refs[4:9]
    fold_place_out, fold_gain_out, up_place_out, up_gain_out, facts = refs[9:]
    core, column, row, plane = place[1], place[2], place[3], place[4]
    for partner, part in zip(PARTNERS, parts):
        facts[pl.ds(2 * jnp.bitwise_xor(column, partner), 2)] = part[...].astype(F32)

    def seed(layer, first):
        high, middle, low = (facts[layer, first + index : first + index + 1, :].astype(jnp.int32) for index in range(3))
        return high * 65536 + middle * 256 + low

    for digit in range(4):
        along_z_out[digit] = facts[0, pl.ds(2 * digit + core, 1), :]
        for pair in range(4):
            even_out[pair, digit] = facts[2 * pair, pl.ds(2 * digit + core, 1), :]
    index = lax.broadcasted_iota(jnp.int32, (16, PIECE), 0)
    gains = jnp.zeros((16, PIECE), F32)
    for pair in range(4):
        gains = jnp.where(index == pair, facts[2 * pair + 1, pl.ds(2 * column + core, 1), :], gains)
    along_y_out[...] = gains.astype(BF)
    even = (row * STEP_P + core * STEP_C) * 16411 + plane * STEP_Q + column * STEP_R
    odd = (column * STEP_R + core * STEP_C) * 16411 + plane * STEP_Q + row * STEP_P
    for layer in range(LAYERS):
        place_out[layer : layer + 1, :] = seed(layer, SEG) * 1000003 + (even if layer % 2 == 0 else odd)
    odd_place = (plane * STEP_Q + column * STEP_R + core * STEP_C) * 16411
    fold_place_out[...] = jnp.broadcast_to(seed(LAYERS - 1, SEG + 3) * 1000003 + odd_place, (SEG, PIECE))
    for digit in range(4):
        fold_gain_out[digit] = facts[LAYERS - 1, pl.ds(16 + SEG * digit + place[0], 1), :]
    block = plane * 4 + row
    for half in range(2):
        chip = facts[pl.ds(2 * column + half, 1)][0]
        high, middle, low = (chip[SEG + 3 + index : SEG + 4 + index].astype(jnp.int32) for index in range(3))
        up_seed = high * 65536 + middle * 256 + low
        up_place_out[half] = jnp.broadcast_to(up_seed * 1000003 + block * (WIDTH * 16411), (SEG, PIECE))
        for digit in range(4):
            index = 16 + SEG * row + 2 * digit + core
            up_gain_out[half, digit] = facts[pl.ds(2 * column + half, 1), pl.ds(index, 1), :][0]
    student_out[...] = jnp.full((SEG, PIECE), student_seed[0] * 1000003 + block * (WIDTH * 16411), jnp.int32)


def squares_tile(squares):
    return split_row(jnp.sum(jnp.transpose(squares), axis=0, keepdims=True))


def embed_kernel(place, token, out, tile_out):
    tokens = jnp.broadcast_to(token[...], (TOK, PIECE)) * 16411 + wrapped(EMBED_KEY * 1000003)
    tokens = tokens + lax.broadcasted_iota(jnp.int32, (TOK, PIECE), 1)
    tokens = tokens + (place[1] * STEP_C + place[3] * STEP_P)
    squares = jnp.zeros((TOK, PIECE), F32)
    for slot, partner in enumerate(PARTNERS):
        for digit in range(4):
            first = jnp.bitwise_xor(place[4], partner) * STEP_Q + digit * STEP_R
            part = hashed(tokens + first, math.sqrt(3.0)).astype(BF)
            out[slot, digit * TOK : (digit + 1) * TOK, :] = part
            wide = part.astype(F32)
            squares = squares + wide * wide
    tile_out[...] = squares_tile(squares)


def first_scale_kernel(embedded, tile, *refs):
    gains, outs = refs[:4], refs[4:]
    for partner in range(4):
        for digit in range(4):
            rows = slice(digit * TOK, (digit + 1) * TOK)
            outs[partner][rows, :] = (embedded[partner, rows, :].astype(F32) * gains[partner][digit]).astype(BF)
        outs[partner][STATE:, :] = tile[...] if partner == 0 else jnp.zeros((16, TOK), BF)


def weight_kernel(layer, plane, place, out):
    chunk = 64
    row_step, col_step = (STEP_R, STEP_P) if layer % 2 == 0 else (STEP_P, STEP_R)
    row = lax.broadcasted_iota(jnp.int32, (chunk, WIDTH), 0)
    col = lax.broadcasted_iota(jnp.int32, (chunk, WIDTH), 1)
    col = (col // 512) * STEP_C + (col // PIECE % 4) * col_step + col % PIECE
    base = row * 16411 + col + jnp.concatenate([place[layer : layer + 1, :]] * (WIDTH // PIECE), axis=1)

    def step(index, carry):
        piece = index // 2
        slot = piece // 4
        partner = jnp.where(slot == 1, PARTNERS[1], jnp.where(slot == 2, PARTNERS[2], slot))
        first = jnp.bitwise_xor(plane[0], partner) * (STEP_Q * 16411) + (piece % 4) * (row_step * 16411) + (index % 2) * (chunk * 16411)
        start = pl.multiple_of(index * chunk, chunk)
        out[pl.ds(start, chunk), :] = hashed(base + first, math.sqrt(3.0 / D)).astype(BF)
        return carry

    lax.fori_loop(0, 2048 // chunk, step, 0, unroll=2)


WEIGHTS = 2048 * WIDTH


def teacher_weight(layer, plane, place):
    body = functools.partial(weight_kernel, layer)
    return call(body, "weight", sds((2048, WIDTH), BF), [SMEM, VMEM], flops=20 * WEIGHTS, nbytes=2 * WEIGHTS)(
        plane, place
    )


def contract_kernel(theirs, core, *refs):
    parts, (weight, *more, out) = refs[:4], refs[4:]
    scaled = [part[digit * TOK : (digit + 1) * TOK, :] for part in parts for digit in range(4)]
    scaled = jnp.concatenate(scaled, axis=1)
    squares = joined_row(parts[0][STATE:, :])
    for part in parts[1:]:
        squares = squares + joined_row(part[STATE:, :])
    out[STATE:GATHER, :] = split_row(squares).astype(out.dtype)
    if more:
        out[GATHER:, :] = more[0][...].astype(out.dtype)
    elif out.shape[0] > GATHER:
        folded = parts[0][GATHER : GATHER + TOK, :].astype(F32)
        for part in parts[1:]:
            folded = folded + part[GATHER : GATHER + TOK, :].astype(F32)
        out[GATHER:, :] = folded.astype(out.dtype)
    first = (1 - core[0] if theirs else core[0]) * STATE
    for pair in range(2):
        columns = pl.ds(pl.multiple_of(first + pair * 256, 256), 256)
        part = jnp.dot(scaled, weight[:, columns], preferred_element_type=F32).astype(out.dtype)
        for half in range(2):
            rows = slice((2 * pair + half) * TOK, (2 * pair + half + 1) * TOK)
            out[rows, :] = part[:, half * PIECE : (half + 1) * PIECE]


def pair_kernel(digit, own, other, stream, *refs):
    *more, out = refs
    total = own[...] + other[...].astype(F32)
    out[:STATE, :] = total[:STATE].astype(BF)
    start = pl.multiple_of(digit[0] * TOK, TOK)
    out[STATE : STATE + TOK, :] = stream[pl.ds(start, TOK), :]
    out[STATE + TOK : SUM, :] = split_row(joined_row(total[STATE:GATHER]))
    if more:
        out[SUM:, :] = more[0][...]
    elif total.shape[0] > GATHER:
        out[SUM:, :] = total[GATHER:].astype(BF)


def placed(digit, parts, out):
    for partner, part in zip(PARTNERS, parts):
        start = pl.multiple_of(jnp.bitwise_xor(digit[0], partner) * TOK, TOK)
        out[pl.ds(start, TOK), :] = part[STATE : STATE + TOK, :]


def pre_kernel(part_a, part_b, part_c, part_d, out):
    wide = [part[GATHER + TOK :, :].astype(F32) for part in (part_a, part_b, part_c, part_d)]
    out[...] = (wide[0] + wide[2]) + (wide[1] + wide[3])


def keep_kernel(digit, part_a, part_b, part_c, part_d, out):
    placed(digit, (part_a, part_b, part_c, part_d), out)


def fold_weight_kernel(place, out):
    base = ternary_base(place)
    for digit in range(4):
        made = ternary(base + digit * (STEP_P * 16411), math.sqrt(1.5 / D))
        out[digit * TOK : (digit + 1) * TOK, :] = made.astype(BF)


def update_kernel(layer, digit, part_a, part_b, part_c, part_d, *refs):
    parts = (part_a, part_b, part_c, part_d)
    following = layer + 1 < LAYERS
    fold = layer + 2 == LAYERS
    if layer == 0:
        stream_out, mean_out, message_out, gains = refs
        for partner, part in zip(PARTNERS, parts):
            for index in range(4):
                row = part[SUM : SUM + 16, :][index : index + 1].astype(F32)
                gains[index, jnp.bitwise_xor(digit[0], partner)] = row
    elif fold:
        gains, fold_weight, fold_gain, stream_out, mean_out, message_out = refs
    elif following:
        gains, stream_out, mean_out, message_out = refs
    else:
        stream_out, mean_out, odd_out, pre_out = refs
    placed(digit, parts, stream_out)

    def total(rows):
        wide = [part[rows, :].astype(F32) for part in parts]
        return (wide[0] + wide[2]) + (wide[1] + wide[3])

    if not following:
        odd_out[...] = stream_out[...]
        pre_out[...] = total(slice(SUM, SUM + TOK))
    squares = joined_row(total(slice(STATE + TOK, SUM)))
    mean = jnp.transpose(jnp.broadcast_to(squares, (TOK, TOK))) * np.float32(1.0 / D)
    mean_out[...] = mean
    scale = lax.rsqrt(mean + EPSILON)
    squares = jnp.zeros((TOK, PIECE), F32)
    folded = jnp.zeros((TOK, R), F32)
    for index in range(4):
        rows = slice(index * TOK, (index + 1) * TOK)
        result = (stream_out[rows, :].astype(F32) + total(rows) * scale).astype(BF)
        stream_out[rows, :] = result
        if following:
            wide = result.astype(F32)
            squares = squares + wide * wide
            message_out[rows, :] = (wide * gains[(layer + 1) // 2, index]).astype(BF)
        if fold:
            scaled = (wide * fold_gain[index]).astype(BF)
            folded = folded + jnp.dot(scaled, fold_weight[rows, :], preferred_element_type=F32)
    if following:
        message_out[STATE:GATHER, :] = squares_tile(squares)
    if fold:
        message_out[GATHER : GATHER + TOK, :] = folded.astype(BF)
        message_out[GATHER + TOK :, :] = total(slice(SUM, SUM + TOK)).astype(BF)


def select_kernel(column, *refs):
    odd, even = refs[:3], refs[3:7]
    odd_out, now_out, later_out, held = refs[7:]
    for index in range(4):
        held[index] = even[index][...]
        held[5 + index] = odd[min(index, 2)][...]
    held[4] = even[3][...]
    odd_out[...] = held[5 + column[0]]
    now_out[...] = held[column[0]]
    later_out[...] = held[column[0] + 1]


def mean_kernel(segment, *refs):
    means, out = refs[:-1], refs[-1]
    mean = means[0][...]
    for layer in range(1, LAYERS - 1):
        mean = jnp.where(segment[0] == layer, means[layer][...], mean)
    out[...] = mean


def swap_kernel(core, column, odd, last_odd, now, later, last, near_out, mine_out):
    end, first = column[0] == 3, core[0] == 0
    later = jnp.where(end, last[...].astype(F32), later[...].astype(F32))
    now = now[...].astype(F32)
    near_out[:STATE, :] = jnp.where(end, last_odd[...].astype(F32), odd[...].astype(F32)).astype(BF)
    near_out[STATE:, :] = jnp.where(first, later, now).astype(BF)
    mine_out[...] = jnp.where(first, now, later).astype(BF)


CORE = [(i, i ^ 1) for i in range(SEG)]
ALONG = {
    "x": ("segment", 2),
    "y": ("mp", 1),
    "z": ("mp", 4),
}


PARTNERS = (0, 2, 1, 3)


def exchange(values, physical):
    axis, step = ALONG[physical]
    size = SEG if axis == "segment" else MP
    values = values if isinstance(values, (list, tuple)) else [values] * 4
    return [values[0]] + [
        lax.ppermute(values[k], axis, [(i, i ^ (k * step)) for i in range(size)]) for k in PARTNERS[1:]
    ]


def summed_along(value, physical):
    own, second, first, third = (part.astype(F32) for part in exchange(value.astype(BF), physical))
    return (own + first) + (second + third)


def ternary_base(place):
    row = lax.broadcasted_iota(jnp.int32, (PIECE, R), 0)
    rank = lax.broadcasted_iota(jnp.int32, (PIECE, R), 1)
    return row * 16411 + rank + place[0:1, :]


def pieces_of(core, index, mine, near, far):
    even = piece_of(core, index, mine, far.at[STATE:])
    odd = piece_of(core, index, near.at[:STATE], far.at[:STATE])
    first = core[0] == 0
    return jnp.where(first, even, odd), jnp.where(first, odd, even)


def piece_of(core, index, here, there):
    first = core[0] == 0
    rows = slice(index // 2 * TOK, (index // 2 + 1) * TOK)
    here, there = here[rows, :].astype(F32), there[rows, :].astype(F32)
    return jnp.where(first, here, there) if index % 2 == 0 else jnp.where(first, there, here)


def student_up_kernel(core, place, gain, now, odd, own_out, other_out):
    totals = []
    for half, stream in enumerate((now, odd)):
        base = ternary_base(place[half]) + core[0] * (STEP_C * 16411)
        total = jnp.zeros((TOK, R), F32)
        for digit in range(4):
            up_weight = ternary(base + digit * (STEP_R * 16411), math.sqrt(1.5 / D)).astype(BF)
            scaled = (stream[digit * TOK : (digit + 1) * TOK, :].astype(F32) * gain[half, digit]).astype(BF)
            total = total + jnp.dot(scaled, up_weight, preferred_element_type=F32)
        totals.append(total)
    first = core[0] == 0
    own_out[...] = jnp.where(first, totals[0], totals[1])
    other_out[...] = jnp.where(first, totals[1], totals[0]).astype(BF)


def student_error_kernel(
    segment, core, place, mine, near, far, pre, last_pre, mean, last_mean, back_out, scaled_out, squared_out, pre_out
):
    base = ternary_base(place) + R
    last = segment[0] == SEG - 1
    scale = lax.rsqrt(jnp.where(last, last_mean[...], mean[...]) + EPSILON)
    rectified = jnp.maximum(jnp.where(last, last_pre[...], pre[...]) * scale, 0.0)
    pre_out[...] = rectified
    squared = (rectified * rectified).astype(BF)
    squared_out[...] = squared
    back = jnp.zeros((TOK, R), F32)
    squares = jnp.zeros((TOK, PIECE), F32)
    for index in range(SEG):
        down_weight = ternary(base + index * PIECE * 16411, math.sqrt(1.5 / R)).astype(BF)
        student = lax.dot_general(squared, down_weight, (((1,), (1,)), ((), ())), preferred_element_type=F32)
        given, target = pieces_of(core, index, mine, near, far)
        error = given + student - target
        squares = squares + error * error
        scaled = (error * np.float32(1.0 / TOK)).astype(BF)
        scaled_out[:, index * PIECE : (index + 1) * PIECE] = scaled
        back = back + jnp.dot(scaled, down_weight, preferred_element_type=F32)
    back_out[:TOK, :] = back.astype(BF)
    back_out[TOK:, :] = jnp.sum(squares.reshape(TOK // 16, 16, PIECE), axis=0).astype(BF)


OVER_TOKENS = (((0,), (0,)), ((), ()))


def student_down_kernel(segment, core, mine, near, far, gain, mean, last_mean, scaled, squared, normed_out, down_out):
    scale = lax.rsqrt(jnp.where(segment[0] == SEG - 1, last_mean[...], mean[...]) + EPSILON)
    for index in range(SEG):
        columns = slice(index * PIECE, (index + 1) * PIECE)
        given, _ = pieces_of(core, index, mine, near, far)
        normed = given * scale * gain[:, columns].astype(F32)
        normed_out[:, columns] = normed.astype(BF)
    down_out[...] = lax.dot_general(scaled[...], squared[...], OVER_TOKENS, preferred_element_type=F32)


def student_grad_kernel(normed, rectified, back, up_out, loss_out):
    back_pre = (back[:TOK, :] * 2.0 * rectified[...]).astype(BF)
    up_out[...] = lax.dot_general(normed[...], back_pre, OVER_TOKENS, preferred_element_type=F32)
    total = jnp.sum(jnp.sum(back[TOK:, :], axis=0, keepdims=True), axis=1, keepdims=True)
    loss_out[...] = total * np.float32(1.0 / (TOK * D))


def local(token_ids, teacher_seeds, student_seeds, teacher_gain, student_gain):
    block = lax.axis_index("mp")
    segment = lax.axis_index("segment")
    core, column = lax.rem(segment, 2), segment // 2
    row, plane = lax.rem(block, 4), block // 4
    place = jnp.stack([segment, core, column, row, plane])
    segment, core, column, row, plane = (part.reshape(1) for part in (segment, core, column, row, plane))
    mean_shape = sds((TOK, TOK), F32)
    state_shape = sds((STATE, PIECE), BF)
    gain_shape = sds((4, 1, PIECE), F32)

    facts = call(pack_kernel, "pack", sds((FACTS, PIECE), BF), [SMEM] * 3 + [VMEM] * 2)(
        teacher_seeds, student_seeds, plane, teacher_gain, student_gain
    )
    facts = call(chip_kernel, "chip", sds((2, FACTS, PIECE), BF), [SMEM, VMEM, VMEM])(
        core, facts, lax.ppermute(facts, "segment", CORE)
    )
    facts = exchange(facts, "x")
    embedded, tile = call(
        embed_kernel, "embed", (sds((4, STATE, PIECE), BF), sds((16, TOK), BF)), [SMEM, VMEM]
    )(place, token_ids.reshape(TOK, 1))
    first_gain, odd_gain, even_gains, places, student_place, fold_place, fold_gain, up_place, up_gain = call(
        facts_kernel,
        "facts",
        (gain_shape, sds((16, PIECE), BF), sds((4, 4, 1, PIECE), F32)) + (sds((LAYERS, PIECE), jnp.int32),) * 3
        + (gain_shape, sds((2, SEG, PIECE), jnp.int32), sds((2, 4, 1, PIECE), F32)),
        [SMEM] * 2 + [VMEM] * 4,
        scratch=(pltpu.VMEM((SEG, FACTS, PIECE), F32),),
    )(place, student_seeds, *facts)
    first_gains = exchange(first_gain, "z")
    weight = teacher_weight(0, plane, places)
    parts = call(
        first_scale_kernel, "first_scale", tuple(sds((GATHER, PIECE), BF) for _ in range(4)), [VMEM] * 6
    )(embedded, tile, *first_gains)
    streams, odd_halves, means = [embedded[0]], [], []
    student_columns = lax.dynamic_slice_in_dim(student_gain, block * WIDTH, WIDTH, 1)
    for layer in range(LAYERS):
        even = layer % 2 == 0
        (axis, digit), other_digit = (("y", row), column) if even else (("x", column), row)
        last = layer + 1 == LAYERS
        if layer:
            parts = exchange(message, "z")
        if layer in (2, 4, 6):
            *parts, odd_halves[-1] = lax.optimization_barrier((*parts, odd_halves[-1]))
        if last:
            weight = teacher_weight(layer, plane, gate(places, message))
        if layer + 2 == LAYERS:
            odd_half, now, later = call(
                select_kernel,
                "select",
                (state_shape,) * 3,
                [SMEM] + [VMEM] * 7,
                scratch=(pltpu.VMEM((9, STATE, PIECE), BF),),
            )(column, *odd_halves, *streams[0:8:2])
            pre_own, pre_other = call(
                student_up_kernel,
                "student_up",
                (sds((TOK, R), F32), sds((TOK, R), BF)),
                [SMEM] + [VMEM] * 4,
                flops=1 << 25,
            )(core, up_place, up_gain, now, odd_half)
            *parts, pre_own, pre_other = lax.optimization_barrier((*parts, pre_own, pre_other))
        if last:
            mean = call(mean_kernel, "mean", mean_shape, [SMEM] + [VMEM] * 7)(segment, *means)
            *parts, mean = lax.optimization_barrier((*parts, mean))
            pre = call(pre_kernel, "pre", sds((TOK, R), F32), [VMEM] * 4)(*parts)
        rows = GATHER + (TOK if layer + 2 >= LAYERS else 0)
        extra = ([pre_other], [pre_own]) if layer + 2 == LAYERS else ([], [])
        contract = dict(in_specs=[SMEM] + [VMEM] * (5 + len(extra[0])), flops=TOK * WEIGHTS, nbytes=2 * WEIGHTS)
        other = call(functools.partial(contract_kernel, True), "contract_other", sds((rows, PIECE), BF), **contract)(
            core, *parts, weight, *extra[0]
        )
        own = call(functools.partial(contract_kernel, False), "contract_own", sds((rows, PIECE), F32), **contract)(
            core, *parts, weight, *extra[1]
        )
        other = lax.ppermute(other, "segment", CORE)
        more = [odd_gain] if layer == 0 else []
        rows = SUM + (16 if layer == 0 else TOK if layer + 2 >= LAYERS else 0)
        summed = call(pair_kernel, "pair", sds((rows, PIECE), BF), [SMEM] + [VMEM] * (3 + len(more)))(
            other_digit, own, other, streams[-1], *more
        )
        parts = exchange(summed, axis)
        out = [state_shape, mean_shape]
        given = [] if layer == 0 or last else [odd_gains if even else even_gains]
        if layer + 2 < LAYERS:
            weight = teacher_weight(layer + 1, plane, gate(places, summed))
            *parts, weight = lax.optimization_barrier((*parts, weight))
        if layer + 2 == LAYERS:
            fold_weight = call(fold_weight_kernel, "fold_weight", state_shape, [VMEM])(gate(fold_place, summed))
            *parts, fold_weight = lax.optimization_barrier((*parts, fold_weight))
            given += [fold_weight, fold_gain]
            out.append(sds((GATHER + 2 * TOK, PIECE), BF))
        elif not last:
            out.append(sds((GATHER, PIECE), BF))
        else:
            out += [state_shape, sds((TOK, R), F32)]
        if layer == 0:
            out.append(sds((4, 4, 1, PIECE), F32))
        stream, stream_mean, *results = call(
            functools.partial(update_kernel, layer), "update", tuple(out), [SMEM] + [VMEM] * (4 + len(given))
        )(digit, *parts, *given)
        if layer in (1, 3, 5):
            odd_halves.append(call(keep_kernel, "keep", state_shape, [SMEM] + [VMEM] * 4)(digit, *parts))
        streams.append(stream)
        if last:
            last_mean, (last_odd, last_pre) = stream_mean, results
        else:
            means.append(stream_mean)
            message = results[0]
        if layer == 0:
            odd_gains = results[1]

    near, mine = call(swap_kernel, "swap", (sds((2 * STATE, PIECE), BF), state_shape), [SMEM] * 2 + [VMEM] * 5)(
        core, column, odd_half, last_odd, now, later, streams[LAYERS]
    )
    far = lax.ppermute(near, "segment", CORE)
    back, scaled, squared, rectified = call(
        student_error_kernel,
        "student_error",
        (sds((TOK + 16, R), BF), sds((TOK, WIDTH), BF), sds((TOK, R), BF), sds((TOK, R), F32)),
        [SMEM] * 2 + [VMEM] * 8,
    )(segment, core, student_place, mine, near, far, pre, last_pre, mean, last_mean)
    normed, grad_down = call(
        student_down_kernel, "student_down", (sds((TOK, WIDTH), BF), sds((WIDTH, R), F32)), [SMEM] * 2 + [VMEM] * 8
    )(segment, core, mine, near, far, student_columns, mean, last_mean, scaled, squared)
    back = summed_along(summed_along(back, "y"), "z")
    grad_up, loss = call(
        student_grad_kernel, "student_grad", (sds((WIDTH, R), F32), sds((1, 1), F32)), [VMEM] * 3
    )(normed, rectified, back)
    return loss.reshape(1), grad_up[None], grad_down[None]


def solution(mesh):
    in_specs = (P(), P("segment"), P("segment"), P("segment", "mp"), P("segment", None))
    out_specs = (P("segment"), P("segment", "mp", None), P("segment", "mp", None))
    return jax.shard_map(local, mesh=mesh, in_specs=in_specs, out_specs=out_specs, check_vma=False)
```

```python
import functools
import math

import jax
import jax.numpy as jnp
import numpy as np
from jax import lax
from jax.experimental import pallas as pl
from jax.experimental.pallas import tpu as pltpu
from jax.sharding import PartitionSpec as P

D = 16384
R = 128
TOK = 128
LAYERS = 8
SEG = 8
MP = 16
WIDTH = D // MP
PIECE = WIDTH // SEG
STATE = 4 * TOK
GATHER = STATE + 16
SUM = STATE + TOK + 16
FACTS = 48
STEP_Q, STEP_P, STEP_R, STEP_C = 4096, 1024, 256, 128
EPSILON = 1e-05
EMBED_KEY = 7919
BF = jnp.bfloat16
F32 = jnp.float32


def wrapped(value):
    value &= 0xFFFFFFFF
    return np.int32(value - (1 << 32) if value >> 31 else value)


MULT = wrapped(73244475)
MULT_SQ = wrapped(73244475 * 73244475)


def fold(bits):
    return jnp.bitwise_xor(bits, lax.shift_right_logical(bits, jnp.int32(16)))


def uniform_bits(mixed_bits):
    mixed_bits = fold(mixed_bits) * MULT
    mixed_bits = fold(mixed_bits) * MULT_SQ
    mixed_bits = fold(mixed_bits) * MULT
    return lax.shift_right_logical(fold(mixed_bits), jnp.int32(8))


def hashed(mixed_bits, magnitude):
    return uniform_bits(mixed_bits).astype(F32) * np.float32(magnitude * 2.0 / 16777216.0) - np.float32(magnitude)


def ternary(mixed_bits, magnitude):
    bits = uniform_bits(mixed_bits)
    return (lax.rem(bits, jnp.int32(3)) - jnp.int32(1)).astype(F32) * np.float32(magnitude)


def split_row(row):
    high = row.astype(BF).astype(F32)
    index = lax.broadcasted_iota(jnp.int32, (16, row.shape[1]), 0)
    tile = jnp.where(index == 0, high, jnp.where(index == 1, row - high, 0.0))
    return tile.astype(BF)


def joined_row(tile):
    return jnp.sum(tile.astype(F32), axis=0, keepdims=True)


SMEM = pl.BlockSpec(memory_space=pltpu.SMEM)
VMEM = pl.BlockSpec(memory_space=pltpu.VMEM)
HBM = pl.BlockSpec(memory_space=pltpu.HBM)


def call(body, name, out_shape, in_specs, flops=0, nbytes=0, limit=8 << 20, out_specs=None, scratch=(), aliases={}):
    single = not isinstance(out_shape, (tuple, list))
    return pl.pallas_call(
        body,
        out_shape=out_shape,
        in_specs=in_specs,
        out_specs=out_specs or (VMEM if single else tuple(VMEM for _ in out_shape)),
        scratch_shapes=scratch,
        input_output_aliases=aliases,
        name=name,
        cost_estimate=pl.CostEstimate(flops=flops, bytes_accessed=nbytes, transcendentals=0),
        compiler_params=pltpu.CompilerParams(vmem_limit_bytes=limit),
    )


def sds(shape, dtype):
    return jax.ShapeDtypeStruct(shape, dtype)


def gate(value, *others):
    return lax.optimization_barrier((value, *others))[0]


def pack_kernel(seed, student_seed, plane, gain_hbm, student_gain_hbm, out, gain, student_gain, sems):
    start = pl.multiple_of(plane[0] * STEP_Q, STEP_Q)
    copies = [
        pltpu.make_async_copy(gain_hbm, gain, sems.at[0]),
        pltpu.make_async_copy(student_gain_hbm.at[:, pl.ds(start, STEP_Q)], student_gain, sems.at[1]),
    ]
    for copy in copies:
        copy.start()
    for copy in copies:
        copy.wait()
    rows = [gain[:, index * PIECE : (index + 1) * PIECE] for index in range(SEG)]
    for value in (seed[0], student_seed[0]):
        for shift in (16, 8, 0):
            byte = jnp.bitwise_and(lax.shift_right_logical(value, jnp.int32(shift)), jnp.int32(255))
            rows.append(jnp.full((1, PIECE), byte, jnp.int32).astype(F32).astype(BF))
    rows += [jnp.zeros((1, PIECE), BF)] * 2
    for index in range(4 * SEG):
        rows.append(student_gain[:, index * PIECE : (index + 1) * PIECE])
    for first in range(0, FACTS, 16):
        out[first : first + 16, :] = jnp.concatenate([row.astype(F32) for row in rows[first : first + 16]], axis=0).astype(BF)


def chip_kernel(core, own, other, out):
    out[core[0]] = own[...]
    out[1 - core[0]] = other[...]


def facts_kernel(place, student_seed, *refs):
    parts, (along_z_out, along_y_out, even_out, place_out, student_out) = refs[:4], refs[4:9]
    fold_place_out, fold_gain_out, up_place_out, up_gain_out, facts = refs[9:]
    core, column, row, plane = place[1], place[2], place[3], place[4]
    for partner, part in zip(SHORT, parts):
        facts[pl.ds(2 * jnp.bitwise_xor(column, partner), 2)] = part[...].astype(F32)

    def seed(layer, first):
        high, middle, low = (facts[layer, first + index : first + index + 1, :].astype(jnp.int32) for index in range(3))
        return high * 65536 + middle * 256 + low

    for digit in range(4):
        along_z_out[digit] = facts[0, pl.ds(2 * digit + core, 1), :]
        for pair in range(4):
            even_out[pair, digit] = facts[2 * pair, pl.ds(2 * digit + core, 1), :]
    index = lax.broadcasted_iota(jnp.int32, (16, PIECE), 0)
    gains = jnp.zeros((16, PIECE), F32)
    for pair in range(4):
        gains = jnp.where(index == pair, facts[2 * pair + 1, pl.ds(2 * column + core, 1), :], gains)
    along_y_out[...] = gains.astype(BF)
    even = (row * STEP_P + core * STEP_C) * 16411 + plane * STEP_Q + column * STEP_R
    odd = (column * STEP_R + core * STEP_C) * 16411 + plane * STEP_Q + row * STEP_P
    for layer in range(LAYERS):
        place_out[layer : layer + 1, :] = seed(layer, SEG) * 1000003 + (even if layer % 2 == 0 else odd)
    odd_place = (plane * STEP_Q + column * STEP_R + core * STEP_C) * 16411
    fold_place_out[...] = jnp.broadcast_to(seed(LAYERS - 1, SEG + 3) * 1000003 + odd_place, (SEG, PIECE))
    for digit in range(4):
        fold_gain_out[digit] = facts[LAYERS - 1, pl.ds(16 + SEG * digit + place[0], 1), :]
    block = plane * 4 + row
    for half in range(2):
        chip = facts[pl.ds(2 * column + half, 1)][0]
        high, middle, low = (chip[SEG + 3 + index : SEG + 4 + index].astype(jnp.int32) for index in range(3))
        up_seed = high * 65536 + middle * 256 + low
        up_place_out[half] = jnp.broadcast_to(up_seed * 1000003 + block * (WIDTH * 16411), (SEG, PIECE))
        for digit in range(4):
            index = 16 + SEG * row + 2 * digit + core
            up_gain_out[half, digit] = facts[pl.ds(2 * column + half, 1), pl.ds(index, 1), :][0]
    student_out[...] = jnp.full((SEG, PIECE), student_seed[0] * 1000003 + block * (WIDTH * 16411), jnp.int32)


def squares_tile(squares):
    return split_row(jnp.sum(jnp.transpose(squares), axis=0, keepdims=True))


def embed_kernel(place, token, out, tile_out):
    tokens = jnp.broadcast_to(token[...], (TOK, PIECE)) * 16411 + wrapped(EMBED_KEY * 1000003)
    tokens = tokens + lax.broadcasted_iota(jnp.int32, (TOK, PIECE), 1)
    tokens = tokens + (place[1] * STEP_C + place[3] * STEP_P)
    squares = jnp.zeros((TOK, PIECE), F32)
    for slot, partner in enumerate(PARTNERS):
        for digit in range(4):
            first = jnp.bitwise_xor(place[4], partner) * STEP_Q + digit * STEP_R
            part = hashed(tokens + first, math.sqrt(3.0)).astype(BF)
            out[slot, digit * TOK : (digit + 1) * TOK, :] = part
            wide = part.astype(F32)
            squares = squares + wide * wide
    tile_out[...] = squares_tile(squares)


def first_scale_kernel(embedded, tile, *refs):
    gains, outs = dict(zip(SHORT, refs[:4])), refs[4:]
    for slot, partner in enumerate(PARTNERS):
        for digit in range(4):
            rows = slice(digit * TOK, (digit + 1) * TOK)
            outs[slot][rows, :] = (embedded[slot, rows, :].astype(F32) * gains[partner][digit]).astype(BF)
        outs[slot][STATE:, :] = tile[...] if slot == 0 else jnp.zeros((16, TOK), BF)


def weight_kernel(layer, plane, place, out):
    chunk = 64
    row_step, col_step = (STEP_R, STEP_P) if layer % 2 == 0 else (STEP_P, STEP_R)
    row = lax.broadcasted_iota(jnp.int32, (chunk, WIDTH), 0)
    col = lax.broadcasted_iota(jnp.int32, (chunk, WIDTH), 1)
    col = (col // 512) * STEP_C + (col // PIECE % 4) * col_step + col % PIECE
    base = row * 16411 + col + jnp.concatenate([place[layer : layer + 1, :]] * (WIDTH // PIECE), axis=1)

    def step(index, carry):
        piece = index // 2
        slot = piece // 4
        partner = jnp.where(slot == 0, 0, jnp.where(slot == 1, PARTNERS[1], jnp.where(slot == 2, PARTNERS[2], PARTNERS[3])))
        first = jnp.bitwise_xor(plane[0], partner) * (STEP_Q * 16411) + (piece % 4) * (row_step * 16411) + (index % 2) * (chunk * 16411)
        start = pl.multiple_of(index * chunk, chunk)
        out[pl.ds(start, chunk), :] = hashed(base + first, math.sqrt(3.0 / D)).astype(BF)
        return carry

    lax.fori_loop(0, 2048 // chunk, step, 0, unroll=2)


WEIGHTS = 2048 * WIDTH


def teacher_weight(layer, plane, place):
    body = functools.partial(weight_kernel, layer)
    return call(body, "weight", sds((2048, WIDTH), BF), [SMEM, VMEM], flops=20 * WEIGHTS, nbytes=2 * WEIGHTS)(
        plane, place
    )


def contract_kernel(theirs, core, *refs):
    parts, (weight, *more, out) = refs[:4], refs[4:]
    scaled = [part[digit * TOK : (digit + 1) * TOK, :] for part in parts for digit in range(4)]
    scaled = jnp.concatenate(scaled, axis=1)
    squares = joined_row(parts[0][STATE:, :])
    for part in parts[1:]:
        squares = squares + joined_row(part[STATE:, :])
    out[STATE:GATHER, :] = split_row(squares).astype(out.dtype)
    if more:
        out[GATHER:, :] = more[0][...].astype(out.dtype)
    elif out.shape[0] > GATHER:
        folded = parts[0][GATHER : GATHER + TOK, :].astype(F32)
        for part in parts[1:]:
            folded = folded + part[GATHER : GATHER + TOK, :].astype(F32)
        out[GATHER:, :] = folded.astype(out.dtype)
    first = (1 - core[0] if theirs else core[0]) * STATE
    for pair in range(2):
        columns = pl.ds(pl.multiple_of(first + pair * 256, 256), 256)
        part = jnp.dot(scaled, weight[:, columns], preferred_element_type=F32).astype(out.dtype)
        for half in range(2):
            rows = slice((2 * pair + half) * TOK, (2 * pair + half + 1) * TOK)
            out[rows, :] = part[:, half * PIECE : (half + 1) * PIECE]


def pair_kernel(digit, own, other, stream, *refs):
    *more, out = refs
    total = own[...] + other[...].astype(F32)
    out[:STATE, :] = total[:STATE].astype(BF)
    start = pl.multiple_of(digit[0] * TOK, TOK)
    out[STATE : STATE + TOK, :] = stream[pl.ds(start, TOK), :]
    out[STATE + TOK : SUM, :] = split_row(joined_row(total[STATE:GATHER]))
    if more:
        out[SUM:, :] = more[0][...]
    elif total.shape[0] > GATHER:
        out[SUM:, :] = total[GATHER:].astype(BF)


def placed(digit, parts, out):
    for partner, part in zip(PARTNERS, parts):
        start = pl.multiple_of(jnp.bitwise_xor(digit[0], partner) * TOK, TOK)
        out[pl.ds(start, TOK), :] = part[STATE : STATE + TOK, :]


def pre_kernel(part_a, part_b, part_c, part_d, out):
    parts = zip(PARTNERS, (part_a, part_b, part_c, part_d))
    wide = {partner: part[GATHER + TOK :, :].astype(F32) for partner, part in parts}
    out[...] = (wide[0] + wide[1]) + (wide[2] + wide[3])


def keep_kernel(digit, part_a, part_b, part_c, part_d, out):
    placed(digit, (part_a, part_b, part_c, part_d), out)


def fold_weight_kernel(place, out):
    base = ternary_base(place)
    for digit in range(4):
        made = ternary(base + digit * (STEP_P * 16411), math.sqrt(1.5 / D))
        out[digit * TOK : (digit + 1) * TOK, :] = made.astype(BF)


def update_kernel(layer, digit, part_a, part_b, part_c, part_d, *refs):
    parts = (part_a, part_b, part_c, part_d)
    following = layer + 1 < LAYERS
    fold = layer + 2 == LAYERS
    if layer == 0:
        stream_out, mean_out, message_out, gains = refs
        for partner, part in zip(PARTNERS, parts):
            for index in range(4):
                row = part[SUM : SUM + 16, :][index : index + 1].astype(F32)
                gains[index, jnp.bitwise_xor(digit[0], partner)] = row
    elif fold:
        gains, fold_weight, fold_gain, stream_out, mean_out, message_out = refs
    elif following:
        gains, stream_out, mean_out, message_out = refs
    else:
        stream_out, mean_out, odd_out, pre_out = refs
    placed(digit, parts, stream_out)

    def total(rows):
        wide = {partner: part[rows, :].astype(F32) for partner, part in zip(PARTNERS, parts)}
        return (wide[0] + wide[1]) + (wide[2] + wide[3])

    if not following:
        odd_out[...] = stream_out[...]
        pre_out[...] = total(slice(SUM, SUM + TOK))
    squares = joined_row(total(slice(STATE + TOK, SUM)))
    mean = jnp.transpose(jnp.broadcast_to(squares, (TOK, TOK))) * np.float32(1.0 / D)
    mean_out[...] = mean
    scale = lax.rsqrt(mean + EPSILON)
    squares = jnp.zeros((TOK, PIECE), F32)
    folded = jnp.zeros((TOK, R), F32)
    for index in range(4):
        rows = slice(index * TOK, (index + 1) * TOK)
        result = (stream_out[rows, :].astype(F32) + total(rows) * scale).astype(BF)
        stream_out[rows, :] = result
        if following:
            wide = result.astype(F32)
            squares = squares + wide * wide
            message_out[rows, :] = (wide * gains[(layer + 1) // 2, index]).astype(BF)
        if fold:
            scaled = (wide * fold_gain[index]).astype(BF)
            folded = folded + jnp.dot(scaled, fold_weight[rows, :], preferred_element_type=F32)
    if following:
        message_out[STATE:GATHER, :] = squares_tile(squares)
    if fold:
        message_out[GATHER : GATHER + TOK, :] = folded.astype(BF)
        message_out[GATHER + TOK :, :] = total(slice(SUM, SUM + TOK)).astype(BF)


def select_kernel(column, *refs):
    odd, even = refs[:3], refs[3:7]
    odd_out, now_out, later_out, held = refs[7:]
    for index in range(4):
        held[index] = even[index][...]
        held[5 + index] = odd[min(index, 2)][...]
    held[4] = even[3][...]
    odd_out[...] = held[5 + column[0]]
    now_out[...] = held[column[0]]
    later_out[...] = held[column[0] + 1]


def mean_kernel(segment, *refs):
    means, out = refs[:-1], refs[-1]
    mean = means[0][...]
    for layer in range(1, LAYERS - 1):
        mean = jnp.where(segment[0] == layer, means[layer][...], mean)
    out[...] = mean


def swap_kernel(core, column, odd, last_odd, now, later, last, near_out, mine_out):
    end, first = column[0] == 3, core[0] == 0
    later = jnp.where(end, last[...].astype(F32), later[...].astype(F32))
    now = now[...].astype(F32)
    near_out[:STATE, :] = jnp.where(end, last_odd[...].astype(F32), odd[...].astype(F32)).astype(BF)
    near_out[STATE:, :] = jnp.where(first, later, now).astype(BF)
    mine_out[...] = jnp.where(first, now, later).astype(BF)


CORE = [(i, i ^ 1) for i in range(SEG)]
ALONG = {
    "x": ("segment", 2),
    "y": ("mp", 1),
    "z": ("mp", 4),
}


PARTNERS = (0, 3, 2, 1)
SHORT = (0, 3, 2, 1)


def exchange(values, physical, order=PARTNERS):
    axis, step = ALONG[physical]
    size = SEG if axis == "segment" else MP
    values = values if isinstance(values, (list, tuple)) else [values] * 4
    return [values[0]] + [
        lax.ppermute(values[k], axis, [(i, i ^ (k * step)) for i in range(size)]) for k in order[1:]
    ]


def sum_kernel(*refs):
    parts, out = dict(zip(SHORT, refs[:4])), refs[4]
    own, first, second, third = (parts[k][...].astype(F32) for k in range(4))
    out[...] = ((own + first) + (second + third)).astype(out.dtype)


def summed_along(value, physical, dtype):
    parts = exchange(value, physical, SHORT)
    return call(sum_kernel, "sum", sds(value.shape, dtype), [VMEM] * 4)(*parts)


def ternary_base(place):
    row = lax.broadcasted_iota(jnp.int32, (PIECE, R), 0)
    rank = lax.broadcasted_iota(jnp.int32, (PIECE, R), 1)
    return row * 16411 + rank + place[0:1, :]


def pieces_of(core, index, mine, near, far):
    even = piece_of(core, index, mine, far.at[STATE:])
    odd = piece_of(core, index, near.at[:STATE], far.at[:STATE])
    first = core[0] == 0
    return jnp.where(first, even, odd), jnp.where(first, odd, even)


def piece_of(core, index, here, there):
    first = core[0] == 0
    rows = slice(index // 2 * TOK, (index // 2 + 1) * TOK)
    here, there = here[rows, :].astype(F32), there[rows, :].astype(F32)
    return jnp.where(first, here, there) if index % 2 == 0 else jnp.where(first, there, here)


def student_up_kernel(core, place, gain, now, odd, own_out, other_out):
    totals = []
    for half, stream in enumerate((now, odd)):
        base = ternary_base(place[half]) + core[0] * (STEP_C * 16411)
        total = jnp.zeros((TOK, R), F32)
        for digit in range(4):
            up_weight = ternary(base + digit * (STEP_R * 16411), math.sqrt(1.5 / D)).astype(BF)
            scaled = (stream[digit * TOK : (digit + 1) * TOK, :].astype(F32) * gain[half, digit]).astype(BF)
            total = total + jnp.dot(scaled, up_weight, preferred_element_type=F32)
        totals.append(total)
    first = core[0] == 0
    own_out[...] = jnp.where(first, totals[0], totals[1])
    other_out[...] = jnp.where(first, totals[1], totals[0]).astype(BF)


def down_weight_kernel(place, out):
    base = ternary_base(place) + R
    for index in range(SEG):
        made = ternary(base + index * PIECE * 16411, math.sqrt(1.5 / R))
        out[index * PIECE : (index + 1) * PIECE, :] = made.astype(BF)


def student_error_kernel(
    segment, core, down_weights, mine, near, far, pre, last_pre, mean, last_mean, back_out, scaled_out, squared_out, pre_out
):
    last = segment[0] == SEG - 1
    scale = lax.rsqrt(jnp.where(last, last_mean[...], mean[...]) + EPSILON)
    rectified = jnp.maximum(jnp.where(last, last_pre[...], pre[...]) * scale, 0.0)
    pre_out[...] = rectified
    squared = (rectified * rectified).astype(BF)
    squared_out[...] = squared
    back = jnp.zeros((TOK, R), F32)
    squares = jnp.zeros((TOK, PIECE), F32)
    for index in range(SEG):
        down_weight = down_weights[index * PIECE : (index + 1) * PIECE, :]
        student = lax.dot_general(squared, down_weight, (((1,), (1,)), ((), ())), preferred_element_type=F32)
        given, target = pieces_of(core, index, mine, near, far)
        error = given + student - target
        squares = squares + error * error
        scaled = (error * np.float32(1.0 / TOK)).astype(BF)
        scaled_out[:, index * PIECE : (index + 1) * PIECE] = scaled
        back = back + jnp.dot(scaled, down_weight, preferred_element_type=F32)
    back_out[:TOK, :] = back.astype(BF)
    back_out[TOK:, :] = jnp.sum(squares.reshape(TOK // 16, 16, PIECE), axis=0).astype(BF)


OVER_TOKENS = (((0,), (0,)), ((), ()))


def student_down_kernel(segment, core, mine, near, far, gain, mean, last_mean, scaled, squared, normed_out, down_out):
    scale = lax.rsqrt(jnp.where(segment[0] == SEG - 1, last_mean[...], mean[...]) + EPSILON)
    for index in range(SEG):
        columns = slice(index * PIECE, (index + 1) * PIECE)
        given, _ = pieces_of(core, index, mine, near, far)
        normed = given * scale * gain[:, columns].astype(F32)
        normed_out[columns, :] = jnp.transpose(normed).astype(BF)
    down_out[...] = lax.dot_general(scaled[...], squared[...], OVER_TOKENS, preferred_element_type=F32)


def student_grad_kernel(normed, rectified, back, up_out, loss_out):
    back_pre = (back[:TOK, :] * 2.0 * rectified[...]).astype(BF)
    up_out[...] = jnp.dot(normed[...], back_pre, preferred_element_type=F32)
    total = jnp.sum(jnp.sum(back[TOK:, :], axis=0, keepdims=True), axis=1, keepdims=True)
    loss_out[...] = total * np.float32(1.0 / (TOK * D))


def local(token_ids, teacher_seeds, student_seeds, teacher_gain, student_gain):
    block = lax.axis_index("mp")
    segment = lax.axis_index("segment")
    core, column = lax.rem(segment, 2), segment // 2
    row, plane = lax.rem(block, 4), block // 4
    place = jnp.stack([segment, core, column, row, plane])
    segment, core, column, row, plane = (part.reshape(1) for part in (segment, core, column, row, plane))
    mean_shape = sds((TOK, TOK), F32)
    state_shape = sds((STATE, PIECE), BF)
    gain_shape = sds((4, 1, PIECE), F32)

    pack_scratch = (pltpu.VMEM((1, WIDTH), BF), pltpu.VMEM((1, STEP_Q), BF), pltpu.SemaphoreType.DMA((2,)))
    facts = call(
        pack_kernel, "pack", sds((FACTS, PIECE), BF), [SMEM] * 3 + [HBM] * 2, scratch=pack_scratch
    )(
        teacher_seeds, student_seeds, plane, teacher_gain, student_gain
    )
    facts = call(chip_kernel, "chip", sds((2, FACTS, PIECE), BF), [SMEM, VMEM, VMEM])(
        core, facts, lax.ppermute(facts, "segment", CORE)
    )
    facts = exchange(facts, "x", SHORT)
    embedded, tile = call(
        embed_kernel, "embed", (sds((4, STATE, PIECE), BF), sds((16, TOK), BF)), [SMEM, VMEM]
    )(place, token_ids.reshape(TOK, 1))
    first_gain, odd_gain, even_gains, places, student_place, fold_place, fold_gain, up_place, up_gain = call(
        facts_kernel,
        "facts",
        (gain_shape, sds((16, PIECE), BF), sds((4, 4, 1, PIECE), F32)) + (sds((LAYERS, PIECE), jnp.int32),) * 3
        + (gain_shape, sds((2, SEG, PIECE), jnp.int32), sds((2, 4, 1, PIECE), F32)),
        [SMEM] * 2 + [VMEM] * 4,
        scratch=(pltpu.VMEM((SEG, FACTS, PIECE), F32),),
    )(place, student_seeds, *facts)
    first_gains = exchange(first_gain, "z", SHORT)
    weight = teacher_weight(0, plane, places)
    parts = call(
        first_scale_kernel, "first_scale", tuple(sds((GATHER, PIECE), BF) for _ in range(4)), [VMEM] * 6
    )(embedded, tile, *first_gains)
    streams, odd_halves, means = [embedded[0]], [], []
    student_columns = lax.dynamic_slice_in_dim(student_gain, block * WIDTH, WIDTH, 1)
    for layer in range(LAYERS):
        even = layer % 2 == 0
        (axis, digit), other_digit = (("y", row), column) if even else (("x", column), row)
        last = layer + 1 == LAYERS
        if layer:
            parts = exchange(message, "z")
        if layer in (2, 4, 6):
            *parts, odd_halves[-1] = lax.optimization_barrier((*parts, odd_halves[-1]))
        if last:
            weight = teacher_weight(layer, plane, gate(places, message))
        if layer + 2 == LAYERS:
            odd_half, now, later = call(
                select_kernel,
                "select",
                (state_shape,) * 3,
                [SMEM] + [VMEM] * 7,
                scratch=(pltpu.VMEM((9, STATE, PIECE), BF),),
            )(column, *odd_halves, *streams[0:8:2])
            pre_own, pre_other = call(
                student_up_kernel,
                "student_up",
                (sds((TOK, R), F32), sds((TOK, R), BF)),
                [SMEM] + [VMEM] * 4,
                flops=1 << 25,
            )(core, up_place, up_gain, now, odd_half)
            *parts, pre_own, pre_other = lax.optimization_barrier((*parts, pre_own, pre_other))
        if last:
            mean = call(mean_kernel, "mean", mean_shape, [SMEM] + [VMEM] * 7)(segment, *means)
            *parts, mean = lax.optimization_barrier((*parts, mean))
            pre = call(pre_kernel, "pre", sds((TOK, R), F32), [VMEM] * 4)(*parts)
        rows = GATHER + (TOK if layer + 2 >= LAYERS else 0)
        extra = ([pre_other], [pre_own]) if layer + 2 == LAYERS else ([], [])
        contract = dict(in_specs=[SMEM] + [VMEM] * (5 + len(extra[0])), flops=TOK * WEIGHTS, nbytes=2 * WEIGHTS)
        other = call(functools.partial(contract_kernel, True), "contract_other", sds((rows, PIECE), BF), **contract)(
            core, *parts, weight, *extra[0]
        )
        own = call(functools.partial(contract_kernel, False), "contract_own", sds((rows, PIECE), F32), **contract)(
            core, *parts, weight, *extra[1]
        )
        other = lax.ppermute(other, "segment", CORE)
        more = [odd_gain] if layer == 0 else []
        rows = SUM + (16 if layer == 0 else TOK if layer + 2 >= LAYERS else 0)
        summed = call(pair_kernel, "pair", sds((rows, PIECE), BF), [SMEM] + [VMEM] * (3 + len(more)))(
            other_digit, own, other, streams[-1], *more
        )
        parts = exchange(summed, axis)
        out = [state_shape, mean_shape]
        given = [] if layer == 0 or last else [odd_gains if even else even_gains]
        if layer + 2 < LAYERS:
            weight = teacher_weight(layer + 1, plane, gate(places, summed))
            *parts, weight = lax.optimization_barrier((*parts, weight))
        if layer + 2 == LAYERS:
            fold_weight = call(fold_weight_kernel, "fold_weight", state_shape, [VMEM])(gate(fold_place, summed))
            *parts, fold_weight = lax.optimization_barrier((*parts, fold_weight))
            given += [fold_weight, fold_gain]
            out.append(sds((GATHER + 2 * TOK, PIECE), BF))
        elif not last:
            out.append(sds((GATHER, PIECE), BF))
        else:
            down_weight = call(down_weight_kernel, "down_weight", sds((WIDTH, R), BF), [VMEM])(
                gate(student_place, summed)
            )
            *parts, down_weight = lax.optimization_barrier((*parts, down_weight))
            out += [state_shape, sds((TOK, R), F32)]
        if layer == 0:
            out.append(sds((4, 4, 1, PIECE), F32))
        stream, stream_mean, *results = call(
            functools.partial(update_kernel, layer), "update", tuple(out), [SMEM] + [VMEM] * (4 + len(given))
        )(digit, *parts, *given)
        if layer in (1, 3, 5):
            odd_halves.append(call(keep_kernel, "keep", state_shape, [SMEM] + [VMEM] * 4)(digit, *parts))
        streams.append(stream)
        if last:
            last_mean, (last_odd, last_pre) = stream_mean, results
        else:
            means.append(stream_mean)
            message = results[0]
        if layer == 0:
            odd_gains = results[1]

    near, mine = call(swap_kernel, "swap", (sds((2 * STATE, PIECE), BF), state_shape), [SMEM] * 2 + [VMEM] * 5)(
        core, column, odd_half, last_odd, now, later, streams[LAYERS]
    )
    far = lax.ppermute(near, "segment", CORE)
    back, scaled, squared, rectified = call(
        student_error_kernel,
        "student_error",
        (sds((TOK + 16, R), BF), sds((TOK, WIDTH), BF), sds((TOK, R), BF), sds((TOK, R), F32)),
        [SMEM] * 2 + [VMEM] * 8,
    )(segment, core, down_weight, mine, near, far, pre, last_pre, mean, last_mean)
    normed, grad_down = call(
        student_down_kernel, "student_down", (sds((WIDTH, TOK), BF), sds((WIDTH, R), F32)), [SMEM] * 2 + [VMEM] * 8
    )(segment, core, mine, near, far, student_columns, mean, last_mean, scaled, squared)
    back = summed_along(summed_along(back, "y", BF), "z", F32)
    grad_up, loss = call(
        student_grad_kernel, "student_grad", (sds((WIDTH, R), F32), sds((1, 1), F32)), [VMEM] * 3
    )(normed, rectified, back)
    return loss.reshape(1), grad_up[None], grad_down[None]


def solution(mesh):
    in_specs = (P(), P("segment"), P("segment"), P("segment", "mp"), P("segment", None))
    out_specs = (P("segment"), P("segment", "mp", None), P("segment", "mp", None))
    return jax.shard_map(local, mesh=mesh, in_specs=in_specs, out_specs=out_specs, check_vma=False)
```

```python
import functools
import math

import jax
import jax.numpy as jnp
import numpy as np
from jax import lax
from jax.experimental import pallas as pl
from jax.experimental.pallas import tpu as pltpu
from jax.sharding import PartitionSpec as P

D = 16384
R = 128
TOK = 128
LAYERS = 8
SEG = 8
MP = 16
WIDTH = D // MP
PIECE = WIDTH // SEG
STATE = 4 * TOK
GATHER = STATE + 16
SUM = STATE + TOK + 16
FACTS = 48
STEP_Q, STEP_P, STEP_R, STEP_C = 4096, 1024, 256, 128
EPSILON = 1e-05
EMBED_KEY = 7919
BF = jnp.bfloat16
F32 = jnp.float32


def wrapped(value):
    value &= 0xFFFFFFFF
    return np.int32(value - (1 << 32) if value >> 31 else value)


MULT = wrapped(73244475)
MULT_SQ = wrapped(73244475 * 73244475)


def fold(bits):
    return jnp.bitwise_xor(bits, lax.shift_right_logical(bits, jnp.int32(16)))


def uniform_bits(mixed_bits):
    mixed_bits = fold(mixed_bits) * MULT
    mixed_bits = fold(mixed_bits) * MULT_SQ
    mixed_bits = fold(mixed_bits) * MULT
    return lax.shift_right_logical(fold(mixed_bits), jnp.int32(8))


def hashed(mixed_bits, magnitude):
    return uniform_bits(mixed_bits).astype(F32) * np.float32(magnitude * 2.0 / 16777216.0) - np.float32(magnitude)


def ternary(mixed_bits, magnitude):
    bits = uniform_bits(mixed_bits)
    return (lax.rem(bits, jnp.int32(3)) - jnp.int32(1)).astype(F32) * np.float32(magnitude)


def split_row(row):
    high = row.astype(BF).astype(F32)
    index = lax.broadcasted_iota(jnp.int32, (16, row.shape[1]), 0)
    tile = jnp.where(index == 0, high, jnp.where(index == 1, row - high, 0.0))
    return tile.astype(BF)


def joined_row(tile):
    return jnp.sum(tile.astype(F32), axis=0, keepdims=True)


SMEM = pl.BlockSpec(memory_space=pltpu.SMEM)
VMEM = pl.BlockSpec(memory_space=pltpu.VMEM)
HBM = pl.BlockSpec(memory_space=pltpu.HBM)


def call(body, name, out_shape, in_specs, flops=0, nbytes=0, limit=8 << 20, out_specs=None, scratch=(), aliases={}):
    single = not isinstance(out_shape, (tuple, list))
    return pl.pallas_call(
        body,
        out_shape=out_shape,
        in_specs=in_specs,
        out_specs=out_specs or (VMEM if single else tuple(VMEM for _ in out_shape)),
        scratch_shapes=scratch,
        input_output_aliases=aliases,
        name=name,
        cost_estimate=pl.CostEstimate(flops=flops, bytes_accessed=nbytes, transcendentals=0),
        compiler_params=pltpu.CompilerParams(vmem_limit_bytes=limit),
    )


def sds(shape, dtype):
    return jax.ShapeDtypeStruct(shape, dtype)


def gate(value, *others):
    return lax.optimization_barrier((value, *others))[0]


def pack_kernel(seed, student_seed, plane, gain_hbm, student_gain_hbm, out, gain, student_gain, sems):
    start = pl.multiple_of(plane[0] * STEP_Q, STEP_Q)
    copies = [
        pltpu.make_async_copy(gain_hbm, gain, sems.at[0]),
        pltpu.make_async_copy(student_gain_hbm.at[:, pl.ds(start, STEP_Q)], student_gain, sems.at[1]),
    ]
    for copy in copies:
        copy.start()
    for copy in copies:
        copy.wait()
    rows = [gain[:, index * PIECE : (index + 1) * PIECE] for index in range(SEG)]
    for value in (seed[0], student_seed[0]):
        for shift in (16, 8, 0):
            byte = jnp.bitwise_and(lax.shift_right_logical(value, jnp.int32(shift)), jnp.int32(255))
            rows.append(jnp.full((1, PIECE), byte, jnp.int32).astype(F32).astype(BF))
    rows += [jnp.zeros((1, PIECE), BF)] * 2
    for index in range(4 * SEG):
        rows.append(student_gain[:, index * PIECE : (index + 1) * PIECE])
    for first in range(0, FACTS, 16):
        out[first : first + 16, :] = jnp.concatenate([row.astype(F32) for row in rows[first : first + 16]], axis=0).astype(BF)


def chip_kernel(core, own, other, out):
    out[core[0]] = own[...]
    out[1 - core[0]] = other[...]


def facts_kernel(place, student_seed, *refs):
    parts, (along_z_out, along_y_out, even_out, place_out, student_out) = refs[:4], refs[4:9]
    fold_place_out, fold_gain_out, up_place_out, up_gain_out, facts = refs[9:]
    core, column, row, plane = place[1], place[2], place[3], place[4]
    for partner, part in zip(SHORT, parts):
        facts[pl.ds(2 * jnp.bitwise_xor(column, partner), 2)] = part[...].astype(F32)

    def seed(layer, first):
        high, middle, low = (facts[layer, first + index : first + index + 1, :].astype(jnp.int32) for index in range(3))
        return high * 65536 + middle * 256 + low

    for digit in range(4):
        along_z_out[digit] = facts[0, pl.ds(2 * digit + core, 1), :]
        for pair in range(4):
            even_out[pair, digit] = facts[2 * pair, pl.ds(2 * digit + core, 1), :]
    index = lax.broadcasted_iota(jnp.int32, (16, PIECE), 0)
    gains = jnp.zeros((16, PIECE), F32)
    for pair in range(4):
        gains = jnp.where(index == pair, facts[2 * pair + 1, pl.ds(2 * column + core, 1), :], gains)
    along_y_out[...] = gains.astype(BF)
    even = (row * STEP_P + core * STEP_C) * 16411 + plane * STEP_Q + column * STEP_R
    odd = (column * STEP_R + core * STEP_C) * 16411 + plane * STEP_Q + row * STEP_P
    for layer in range(LAYERS):
        place_out[layer : layer + 1, :] = seed(layer, SEG) * 1000003 + (even if layer % 2 == 0 else odd)
    odd_place = (plane * STEP_Q + column * STEP_R + core * STEP_C) * 16411
    fold_place_out[...] = jnp.broadcast_to(seed(LAYERS - 1, SEG + 3) * 1000003 + odd_place, (SEG, PIECE))
    for digit in range(4):
        fold_gain_out[digit] = facts[LAYERS - 1, pl.ds(16 + SEG * digit + place[0], 1), :]
    block = plane * 4 + row
    for half in range(2):
        chip = facts[pl.ds(2 * column + half, 1)][0]
        high, middle, low = (chip[SEG + 3 + index : SEG + 4 + index].astype(jnp.int32) for index in range(3))
        up_seed = high * 65536 + middle * 256 + low
        up_place_out[half] = jnp.broadcast_to(up_seed * 1000003 + block * (WIDTH * 16411), (SEG, PIECE))
        for digit in range(4):
            index = 16 + SEG * row + 2 * digit + core
            up_gain_out[half, digit] = facts[pl.ds(2 * column + half, 1), pl.ds(index, 1), :][0]
    student_out[...] = jnp.full((SEG, PIECE), student_seed[0] * 1000003 + block * (WIDTH * 16411), jnp.int32)


def squares_tile(squares):
    return split_row(jnp.sum(jnp.transpose(squares), axis=0, keepdims=True))


def embed_kernel(place, token, out, tile_out, before_out):
    tokens = jnp.broadcast_to(token[...], (TOK, PIECE)) * 16411 + wrapped(EMBED_KEY * 1000003)
    tokens = tokens + lax.broadcasted_iota(jnp.int32, (TOK, PIECE), 1)
    tokens = tokens + (place[1] * STEP_C + place[3] * STEP_P)
    squares = jnp.zeros((TOK, PIECE), F32)
    for slot, partner in enumerate(SLOTS):
        for digit in range(4):
            first = jnp.bitwise_xor(place[4], partner) * STEP_Q + digit * STEP_R
            part = hashed(tokens + first, math.sqrt(3.0)).astype(BF)
            out[slot, digit * TOK : (digit + 1) * TOK, :] = part
            wide = part.astype(F32)
            squares = squares + wide * wide
    tile_out[...] = squares_tile(squares)
    tokens = tokens + (place[2] * STEP_R + place[4] * STEP_Q - place[3] * STEP_P)
    for digit in range(4):
        rows = slice(digit * TOK, (digit + 1) * TOK)
        before_out[rows, :] = hashed(tokens + digit * STEP_P, math.sqrt(3.0)).astype(BF)


def first_scale_kernel(embedded, tile, *refs):
    gains, outs = dict(zip(SHORT, refs[:4])), refs[4:]
    for slot, partner in enumerate(SLOTS):
        for digit in range(4):
            rows = slice(digit * TOK, (digit + 1) * TOK)
            outs[slot][rows, :] = (embedded[slot, rows, :].astype(F32) * gains[partner][digit]).astype(BF)
        outs[slot][STATE:, :] = tile[...] if slot == 0 else jnp.zeros((16, TOK), BF)


def weight_kernel(layer, plane, place, out):
    chunk = 64
    row_step, col_step = (STEP_R, STEP_P) if layer % 2 == 0 else (STEP_P, STEP_R)
    row = lax.broadcasted_iota(jnp.int32, (chunk, WIDTH), 0)
    col = lax.broadcasted_iota(jnp.int32, (chunk, WIDTH), 1)
    col = (col // 512) * STEP_C + (col // PIECE % 4) * col_step + col % PIECE
    base = row * 16411 + col + jnp.concatenate([place[layer : layer + 1, :]] * (WIDTH // PIECE), axis=1)

    def step(index, carry):
        piece = index // 2
        slot = piece // 4
        partner = jnp.where(slot == 0, 0, jnp.where(slot == 1, SLOTS[1], jnp.where(slot == 2, SLOTS[2], SLOTS[3])))
        first = jnp.bitwise_xor(plane[0], partner) * (STEP_Q * 16411) + (piece % 4) * (row_step * 16411) + (index % 2) * (chunk * 16411)
        start = pl.multiple_of(index * chunk, chunk)
        out[pl.ds(start, chunk), :] = hashed(base + first, math.sqrt(3.0 / D)).astype(BF)
        return carry

    lax.fori_loop(0, 2048 // chunk, step, 0, unroll=2)


WEIGHTS = 2048 * WIDTH


def teacher_weight(layer, plane, place):
    body = functools.partial(weight_kernel, layer)
    return call(body, "weight", sds((2048, WIDTH), BF), [SMEM, VMEM], flops=20 * WEIGHTS, nbytes=2 * WEIGHTS)(
        plane, place
    )


BEGUN = 1536


def rows_of(parts):
    return jnp.concatenate([part[digit * TOK : (digit + 1) * TOK, :] for part in parts for digit in range(4)], axis=1)


def begin_kernel(core, part_a, part_b, part_c, weight, their_out, own_out):
    scaled = rows_of((part_a, part_b, part_c))
    for first, out in (((1 - core[0]) * STATE, their_out), (core[0] * STATE, own_out)):
        for pair in range(2):
            columns = pl.ds(pl.multiple_of(first + pair * 256, 256), 256)
            part = jnp.dot(scaled, weight[:BEGUN, columns], preferred_element_type=F32)
            for half in range(2):
                rows = slice((2 * pair + half) * TOK, (2 * pair + half + 1) * TOK)
                out[rows, :] = part[:, half * PIECE : (half + 1) * PIECE]


def contract_kernel(theirs, core, *refs):
    parts, (weight, begun, *more, out) = refs[:4], refs[4:]
    scaled = rows_of(parts[3:])
    squares = joined_row(parts[0][STATE:, :])
    for part in parts[1:]:
        squares = squares + joined_row(part[STATE:, :])
    out[STATE:GATHER, :] = split_row(squares).astype(out.dtype)
    if more:
        out[GATHER:, :] = more[0][...].astype(out.dtype)
    elif out.shape[0] > GATHER:
        folded = parts[0][GATHER : GATHER + TOK, :].astype(F32)
        for part in parts[1:]:
            folded = folded + part[GATHER : GATHER + TOK, :].astype(F32)
        out[GATHER:, :] = folded.astype(out.dtype)
    first = (1 - core[0] if theirs else core[0]) * STATE
    for pair in range(2):
        columns = pl.ds(pl.multiple_of(first + pair * 256, 256), 256)
        part = jnp.dot(scaled, weight[BEGUN:, columns], preferred_element_type=F32)
        for half in range(2):
            rows = slice((2 * pair + half) * TOK, (2 * pair + half + 1) * TOK)
            out[rows, :] = (begun[rows, :] + part[:, half * PIECE : (half + 1) * PIECE]).astype(out.dtype)


def pair_kernel(digit, own, other, stream, *refs):
    *more, out = refs
    total = own[...] + other[...].astype(F32)
    out[:STATE, :] = total[:STATE].astype(BF)
    if more:
        out[STATE:GATHER, :] = split_row(joined_row(total[STATE:GATHER]))
        out[GATHER:, :] = more[0][...]
        return
    start = pl.multiple_of(digit[0] * TOK, TOK)
    out[STATE : STATE + TOK, :] = stream[pl.ds(start, TOK), :]
    out[STATE + TOK : SUM, :] = split_row(joined_row(total[STATE:GATHER]))
    if total.shape[0] > GATHER:
        out[SUM:, :] = total[GATHER:].astype(BF)


def placed(digit, parts, out):
    for partner, part in zip(PARTNERS, parts):
        start = pl.multiple_of(jnp.bitwise_xor(digit[0], partner) * TOK, TOK)
        out[pl.ds(start, TOK), :] = part[STATE : STATE + TOK, :]


def pre_kernel(part_a, part_b, part_c, part_d, out):
    parts = zip(SLOTS, (part_a, part_b, part_c, part_d))
    wide = {partner: part[GATHER + TOK :, :].astype(F32) for partner, part in parts}
    out[...] = (wide[0] + wide[1]) + (wide[2] + wide[3])


def keep_kernel(digit, part_a, part_b, part_c, part_d, out):
    placed(digit, (part_a, part_b, part_c, part_d), out)


def fold_weight_kernel(place, out):
    base = ternary_base(place)
    for digit in range(4):
        made = ternary(base + digit * (STEP_P * 16411), math.sqrt(1.5 / D))
        out[digit * TOK : (digit + 1) * TOK, :] = made.astype(BF)


def update_kernel(layer, digit, part_a, part_b, part_c, part_d, *refs):
    parts = (part_a, part_b, part_c, part_d)
    following = layer + 1 < LAYERS
    fold = layer + 2 == LAYERS
    if layer == 0:
        before, stream_out, mean_out, message_out, gains = refs
        for partner, part in zip(PARTNERS, parts):
            for index in range(4):
                row = part[GATHER : GATHER + 16, :][index : index + 1].astype(F32)
                gains[index, jnp.bitwise_xor(digit[0], partner)] = row
    elif fold:
        gains, fold_weight, fold_gain, stream_out, mean_out, message_out = refs
    elif following:
        gains, stream_out, mean_out, message_out = refs
    else:
        stream_out, mean_out, odd_out, pre_out = refs
    if layer:
        placed(digit, parts, stream_out)
    else:
        stream_out[...] = before[...]

    def total(rows):
        wide = {partner: part[rows, :].astype(F32) for partner, part in zip(PARTNERS, parts)}
        return (wide[0] + wide[1]) + (wide[2] + wide[3])

    if not following:
        odd_out[...] = stream_out[...]
        pre_out[...] = total(slice(SUM, SUM + TOK))
    squares = joined_row(total(slice(STATE + TOK, SUM) if layer else slice(STATE, GATHER)))
    mean = jnp.transpose(jnp.broadcast_to(squares, (TOK, TOK))) * np.float32(1.0 / D)
    mean_out[...] = mean
    scale = lax.rsqrt(mean + EPSILON)
    squares = jnp.zeros((TOK, PIECE), F32)
    folded = jnp.zeros((TOK, R), F32)
    for index in range(4):
        rows = slice(index * TOK, (index + 1) * TOK)
        result = (stream_out[rows, :].astype(F32) + total(rows) * scale).astype(BF)
        stream_out[rows, :] = result
        if following:
            wide = result.astype(F32)
            squares = squares + wide * wide
            message_out[rows, :] = (wide * gains[(layer + 1) // 2, index]).astype(BF)
        if fold:
            scaled = (wide * fold_gain[index]).astype(BF)
            folded = folded + jnp.dot(scaled, fold_weight[rows, :], preferred_element_type=F32)
    if following:
        message_out[STATE:GATHER, :] = squares_tile(squares)
    if fold:
        message_out[GATHER : GATHER + TOK, :] = folded.astype(BF)
        message_out[GATHER + TOK :, :] = total(slice(SUM, SUM + TOK)).astype(BF)


def select_kernel(column, *refs):
    odd, even = refs[:3], refs[3:7]
    odd_out, now_out, later_out, held = refs[7:]
    for index in range(4):
        held[index] = even[index][...]
        held[5 + index] = odd[min(index, 2)][...]
    held[4] = even[3][...]
    odd_out[...] = held[5 + column[0]]
    now_out[...] = held[column[0]]
    later_out[...] = held[column[0] + 1]


def mean_kernel(segment, *refs):
    means, out = refs[:-1], refs[-1]
    mean = means[0][...]
    for layer in range(1, LAYERS - 1):
        mean = jnp.where(segment[0] == layer, means[layer][...], mean)
    out[...] = mean


def swap_kernel(core, column, odd, last_odd, now, later, last, near_out, mine_out):
    end, first = column[0] == 3, core[0] == 0
    later = jnp.where(end, last[...].astype(F32), later[...].astype(F32))
    now = now[...].astype(F32)
    near_out[:STATE, :] = jnp.where(end, last_odd[...].astype(F32), odd[...].astype(F32)).astype(BF)
    near_out[STATE:, :] = jnp.where(first, later, now).astype(BF)
    mine_out[...] = jnp.where(first, now, later).astype(BF)


CORE = [(i, i ^ 1) for i in range(SEG)]
ALONG = {
    "x": ("segment", 2),
    "y": ("mp", 1),
    "z": ("mp", 4),
}


PARTNERS = (0, 3, 2, 1)
SLOTS = (0, 3, 1, 2)
SHORT = (0, 3, 2, 1)


def exchange(values, physical, order=PARTNERS):
    axis, step = ALONG[physical]
    size = SEG if axis == "segment" else MP
    values = values if isinstance(values, (list, tuple)) else [values] * 4
    return [values[0]] + [
        lax.ppermute(values[k], axis, [(i, i ^ (k * step)) for i in range(size)]) for k in order[1:]
    ]


def sum_kernel(*refs):
    parts, out = dict(zip(SHORT, refs[:4])), refs[4]
    own, first, second, third = (parts[k][...].astype(F32) for k in range(4))
    out[...] = ((own + first) + (second + third)).astype(out.dtype)


def summed_along(value, physical, dtype):
    parts = exchange(value, physical, SHORT)
    return call(sum_kernel, "sum", sds(value.shape, dtype), [VMEM] * 4)(*parts)


def ternary_base(place):
    row = lax.broadcasted_iota(jnp.int32, (PIECE, R), 0)
    rank = lax.broadcasted_iota(jnp.int32, (PIECE, R), 1)
    return row * 16411 + rank + place[0:1, :]


def pieces_of(core, index, mine, near, far):
    even = piece_of(core, index, mine, far.at[STATE:])
    odd = piece_of(core, index, near.at[:STATE], far.at[:STATE])
    first = core[0] == 0
    return jnp.where(first, even, odd), jnp.where(first, odd, even)


def piece_of(core, index, here, there):
    first = core[0] == 0
    rows = slice(index // 2 * TOK, (index // 2 + 1) * TOK)
    here, there = here[rows, :].astype(F32), there[rows, :].astype(F32)
    return jnp.where(first, here, there) if index % 2 == 0 else jnp.where(first, there, here)


def student_up_kernel(core, place, gain, now, odd, own_out, other_out):
    totals = []
    for half, stream in enumerate((now, odd)):
        base = ternary_base(place[half]) + core[0] * (STEP_C * 16411)
        total = jnp.zeros((TOK, R), F32)
        for digit in range(4):
            up_weight = ternary(base + digit * (STEP_R * 16411), math.sqrt(1.5 / D)).astype(BF)
            scaled = (stream[digit * TOK : (digit + 1) * TOK, :].astype(F32) * gain[half, digit]).astype(BF)
            total = total + jnp.dot(scaled, up_weight, preferred_element_type=F32)
        totals.append(total)
    first = core[0] == 0
    own_out[...] = jnp.where(first, totals[0], totals[1])
    other_out[...] = jnp.where(first, totals[1], totals[0]).astype(BF)


def down_weight_kernel(place, out):
    base = ternary_base(place) + R
    for index in range(SEG):
        made = ternary(base + index * PIECE * 16411, math.sqrt(1.5 / R))
        out[index * PIECE : (index + 1) * PIECE, :] = made.astype(BF)


def student_error_kernel(
    segment, core, down_weights, mine, near, far, pre, last_pre, mean, last_mean, back_out, scaled_out, squared_out, pre_out
):
    last = segment[0] == SEG - 1
    scale = lax.rsqrt(jnp.where(last, last_mean[...], mean[...]) + EPSILON)
    rectified = jnp.maximum(jnp.where(last, last_pre[...], pre[...]) * scale, 0.0)
    pre_out[...] = rectified
    squared = (rectified * rectified).astype(BF)
    squared_out[...] = squared
    back = jnp.zeros((TOK, R), F32)
    squares = jnp.zeros((TOK, PIECE), F32)
    for index in range(SEG):
        down_weight = down_weights[index * PIECE : (index + 1) * PIECE, :]
        student = lax.dot_general(squared, down_weight, (((1,), (1,)), ((), ())), preferred_element_type=F32)
        given, target = pieces_of(core, index, mine, near, far)
        error = given + student - target
        squares = squares + error * error
        scaled = (error * np.float32(1.0 / TOK)).astype(BF)
        scaled_out[:, index * PIECE : (index + 1) * PIECE] = scaled
        back = back + jnp.dot(scaled, down_weight, preferred_element_type=F32)
    back_out[:TOK, :] = back.astype(BF)
    back_out[TOK:, :] = jnp.sum(squares.reshape(TOK // 16, 16, PIECE), axis=0).astype(BF)


OVER_TOKENS = (((0,), (0,)), ((), ()))


def student_down_kernel(segment, core, mine, near, far, gain, mean, last_mean, scaled, squared, normed_out, down_out):
    scale = lax.rsqrt(jnp.where(segment[0] == SEG - 1, last_mean[...], mean[...]) + EPSILON)
    for index in range(SEG):
        columns = slice(index * PIECE, (index + 1) * PIECE)
        given, _ = pieces_of(core, index, mine, near, far)
        normed = given * scale * gain[:, columns].astype(F32)
        normed_out[columns, :] = jnp.transpose(normed).astype(BF)
    down_out[...] = lax.dot_general(scaled[...], squared[...], OVER_TOKENS, preferred_element_type=F32)


def student_grad_kernel(normed, rectified, back, up_out, loss_out):
    back_pre = (back[:TOK, :] * 2.0 * rectified[...]).astype(BF)
    up_out[...] = jnp.dot(normed[...], back_pre, preferred_element_type=F32)
    total = jnp.sum(jnp.sum(back[TOK:, :], axis=0, keepdims=True), axis=1, keepdims=True)
    loss_out[...] = total * np.float32(1.0 / (TOK * D))


def local(token_ids, teacher_seeds, student_seeds, teacher_gain, student_gain):
    block = lax.axis_index("mp")
    segment = lax.axis_index("segment")
    core, column = lax.rem(segment, 2), segment // 2
    row, plane = lax.rem(block, 4), block // 4
    place = jnp.stack([segment, core, column, row, plane])
    segment, core, column, row, plane = (part.reshape(1) for part in (segment, core, column, row, plane))
    mean_shape = sds((TOK, TOK), F32)
    state_shape = sds((STATE, PIECE), BF)
    gain_shape = sds((4, 1, PIECE), F32)

    pack_scratch = (pltpu.VMEM((1, WIDTH), BF), pltpu.VMEM((1, STEP_Q), BF), pltpu.SemaphoreType.DMA((2,)))
    facts = call(
        pack_kernel, "pack", sds((FACTS, PIECE), BF), [SMEM] * 3 + [HBM] * 2, scratch=pack_scratch
    )(
        teacher_seeds, student_seeds, plane, teacher_gain, student_gain
    )
    facts = call(chip_kernel, "chip", sds((2, FACTS, PIECE), BF), [SMEM, VMEM, VMEM])(
        core, facts, lax.ppermute(facts, "segment", CORE)
    )
    facts = exchange(facts, "x", SHORT)
    embedded, tile, before = call(
        embed_kernel, "embed", (sds((4, STATE, PIECE), BF), sds((16, TOK), BF), state_shape), [SMEM, VMEM]
    )(place, token_ids.reshape(TOK, 1))
    first_gain, odd_gain, even_gains, places, student_place, fold_place, fold_gain, up_place, up_gain = call(
        facts_kernel,
        "facts",
        (gain_shape, sds((16, PIECE), BF), sds((4, 4, 1, PIECE), F32)) + (sds((LAYERS, PIECE), jnp.int32),) * 3
        + (gain_shape, sds((2, SEG, PIECE), jnp.int32), sds((2, 4, 1, PIECE), F32)),
        [SMEM] * 2 + [VMEM] * 4,
        scratch=(pltpu.VMEM((SEG, FACTS, PIECE), F32),),
    )(place, student_seeds, *facts)
    first_gains = exchange(first_gain, "z", SHORT)
    weight = teacher_weight(0, plane, places)
    parts = call(
        first_scale_kernel, "first_scale", tuple(sds((GATHER, PIECE), BF) for _ in range(4)), [VMEM] * 6
    )(embedded, tile, *first_gains)
    streams, odd_halves, means = [embedded[0]], [], []
    student_columns = lax.dynamic_slice_in_dim(student_gain, block * WIDTH, WIDTH, 1)
    for layer in range(LAYERS):
        even = layer % 2 == 0
        (axis, digit), other_digit = (("y", row), column) if even else (("x", column), row)
        last = layer + 1 == LAYERS
        if layer:
            arrived = dict(zip(PARTNERS, exchange(message, "z")))
            parts = [arrived[partner] for partner in SLOTS]
        if layer in (2, 4, 6):
            parts[3], odd_halves[-1] = lax.optimization_barrier((parts[3], odd_halves[-1]))
        if last:
            weight = teacher_weight(layer, plane, gate(places, message))
        if layer + 2 == LAYERS:
            odd_half, now, later = call(
                select_kernel,
                "select",
                (state_shape,) * 3,
                [SMEM] + [VMEM] * 7,
                scratch=(pltpu.VMEM((9, STATE, PIECE), BF),),
            )(column, *odd_halves, *streams[0:8:2])
            pre_own, pre_other = call(
                student_up_kernel,
                "student_up",
                (sds((TOK, R), F32), sds((TOK, R), BF)),
                [SMEM] + [VMEM] * 4,
                flops=1 << 25,
            )(core, up_place, up_gain, now, odd_half)
            parts[3], pre_own, pre_other = lax.optimization_barrier((parts[3], pre_own, pre_other))
        if last:
            mean = call(mean_kernel, "mean", mean_shape, [SMEM] + [VMEM] * 7)(segment, *means)
            parts[3], mean = lax.optimization_barrier((parts[3], mean))
            pre = call(pre_kernel, "pre", sds((TOK, R), F32), [VMEM] * 4)(*parts)
        rows = GATHER + (TOK if layer + 2 >= LAYERS else 0)
        extra = ([pre_other], [pre_own]) if layer + 2 == LAYERS else ([], [])
        begun = call(
            begin_kernel,
            "begin",
            (sds((STATE, PIECE), F32),) * 2,
            [SMEM] + [VMEM] * 4,
            flops=2 * TOK * WEIGHTS,
            nbytes=2 * WEIGHTS,
        )(core, *parts[:3], weight)
        contract = dict(in_specs=[SMEM] + [VMEM] * (6 + len(extra[0])), flops=TOK * WEIGHTS // 4, nbytes=WEIGHTS // 2)
        other = call(functools.partial(contract_kernel, True), "contract_other", sds((rows, PIECE), BF), **contract)(
            core, *parts, weight, begun[0], *extra[0]
        )
        own = call(functools.partial(contract_kernel, False), "contract_own", sds((rows, PIECE), F32), **contract)(
            core, *parts, weight, begun[1], *extra[1]
        )
        other = lax.ppermute(other, "segment", CORE)
        more = [odd_gain] if layer == 0 else []
        rows = GATHER + 16 if layer == 0 else SUM + (TOK if layer + 2 >= LAYERS else 0)
        summed = call(pair_kernel, "pair", sds((rows, PIECE), BF), [SMEM] + [VMEM] * (3 + len(more)))(
            other_digit, own, other, streams[-1], *more
        )
        parts = exchange(summed, axis)
        out = [state_shape, mean_shape]
        given = [before] if layer == 0 else [] if last else [odd_gains if even else even_gains]
        if layer + 2 < LAYERS:
            weight = teacher_weight(layer + 1, plane, gate(places, summed))
            *parts, weight = lax.optimization_barrier((*parts, weight))
        if layer + 2 == LAYERS:
            fold_weight = call(fold_weight_kernel, "fold_weight", state_shape, [VMEM])(gate(fold_place, summed))
            *parts, fold_weight = lax.optimization_barrier((*parts, fold_weight))
            given += [fold_weight, fold_gain]
            out.append(sds((GATHER + 2 * TOK, PIECE), BF))
        elif not last:
            out.append(sds((GATHER, PIECE), BF))
        else:
            down_weight = call(down_weight_kernel, "down_weight", sds((WIDTH, R), BF), [VMEM])(
                gate(student_place, summed)
            )
            *parts, down_weight = lax.optimization_barrier((*parts, down_weight))
            out += [state_shape, sds((TOK, R), F32)]
        if layer == 0:
            out.append(sds((4, 4, 1, PIECE), F32))
        stream, stream_mean, *results = call(
            functools.partial(update_kernel, layer), "update", tuple(out), [SMEM] + [VMEM] * (4 + len(given))
        )(digit, *parts, *given)
        if layer in (1, 3, 5):
            odd_halves.append(call(keep_kernel, "keep", state_shape, [SMEM] + [VMEM] * 4)(digit, *parts))
        streams.append(stream)
        if last:
            last_mean, (last_odd, last_pre) = stream_mean, results
        else:
            means.append(stream_mean)
            message = results[0]
        if layer == 0:
            odd_gains = results[1]

    near, mine = call(swap_kernel, "swap", (sds((2 * STATE, PIECE), BF), state_shape), [SMEM] * 2 + [VMEM] * 5)(
        core, column, odd_half, last_odd, now, later, streams[LAYERS]
    )
    far = lax.ppermute(near, "segment", CORE)
    back, scaled, squared, rectified = call(
        student_error_kernel,
        "student_error",
        (sds((TOK + 16, R), BF), sds((TOK, WIDTH), BF), sds((TOK, R), BF), sds((TOK, R), F32)),
        [SMEM] * 2 + [VMEM] * 8,
    )(segment, core, down_weight, mine, near, far, pre, last_pre, mean, last_mean)
    normed, grad_down = call(
        student_down_kernel, "student_down", (sds((WIDTH, TOK), BF), sds((WIDTH, R), F32)), [SMEM] * 2 + [VMEM] * 8
    )(segment, core, mine, near, far, student_columns, mean, last_mean, scaled, squared)
    back = summed_along(summed_along(back, "y", BF), "z", F32)
    grad_up, loss = call(
        student_grad_kernel, "student_grad", (sds((WIDTH, R), F32), sds((1, 1), F32)), [VMEM] * 3
    )(normed, rectified, back)
    return loss.reshape(1), grad_up[None], grad_down[None]


def solution(mesh):
    in_specs = (P(), P("segment"), P("segment"), P("segment", "mp"), P("segment", None))
    out_specs = (P("segment"), P("segment", "mp", None), P("segment", "mp", None))
    return jax.shard_map(local, mesh=mesh, in_specs=in_specs, out_specs=out_specs, check_vma=False)
```

```python
import functools
import math

import jax
import jax.numpy as jnp
import numpy as np
from jax import lax
from jax.experimental import pallas as pl
from jax.experimental.pallas import tpu as pltpu
from jax.sharding import PartitionSpec as P

D = 16384
R = 128
TOK = 128
LAYERS = 8
SEG = 8
MP = 16
WIDTH = D // MP
PIECE = WIDTH // SEG
STATE = 4 * TOK
GATHER = STATE + 16
SUM = STATE + TOK + 16
FACTS = 48
STEP_Q, STEP_P, STEP_R, STEP_C = 4096, 1024, 256, 128
EPSILON = 1e-05
EMBED_KEY = 7919
BF = jnp.bfloat16
F32 = jnp.float32


def wrapped(value):
    value &= 0xFFFFFFFF
    return np.int32(value - (1 << 32) if value >> 31 else value)


MULT = wrapped(73244475)
MULT_SQ = wrapped(73244475 * 73244475)


def fold(bits):
    return jnp.bitwise_xor(bits, lax.shift_right_logical(bits, jnp.int32(16)))


def uniform_bits(mixed_bits):
    mixed_bits = fold(mixed_bits) * MULT
    mixed_bits = fold(mixed_bits) * MULT_SQ
    mixed_bits = fold(mixed_bits) * MULT
    return lax.shift_right_logical(fold(mixed_bits), jnp.int32(8))


def hashed(mixed_bits, magnitude):
    return uniform_bits(mixed_bits).astype(F32) * np.float32(magnitude * 2.0 / 16777216.0) - np.float32(magnitude)


def ternary(mixed_bits, magnitude):
    bits = uniform_bits(mixed_bits)
    return (lax.rem(bits, jnp.int32(3)) - jnp.int32(1)).astype(F32) * np.float32(magnitude)


def split_row(row):
    high = row.astype(BF).astype(F32)
    index = lax.broadcasted_iota(jnp.int32, (16, row.shape[1]), 0)
    tile = jnp.where(index == 0, high, jnp.where(index == 1, row - high, 0.0))
    return tile.astype(BF)


def joined_row(tile):
    return jnp.sum(tile.astype(F32), axis=0, keepdims=True)


SMEM = pl.BlockSpec(memory_space=pltpu.SMEM)
VMEM = pl.BlockSpec(memory_space=pltpu.VMEM)
HBM = pl.BlockSpec(memory_space=pltpu.HBM)


def call(body, name, out_shape, in_specs, flops=0, nbytes=0, limit=8 << 20, out_specs=None, scratch=(), aliases={}):
    single = not isinstance(out_shape, (tuple, list))
    return pl.pallas_call(
        body,
        out_shape=out_shape,
        in_specs=in_specs,
        out_specs=out_specs or (VMEM if single else tuple(VMEM for _ in out_shape)),
        scratch_shapes=scratch,
        input_output_aliases=aliases,
        name=name,
        cost_estimate=pl.CostEstimate(flops=flops, bytes_accessed=nbytes, transcendentals=0),
        compiler_params=pltpu.CompilerParams(vmem_limit_bytes=limit),
    )


def sds(shape, dtype):
    return jax.ShapeDtypeStruct(shape, dtype)


def gate(value, *others):
    return lax.optimization_barrier((value, *others))[0]


def pack_kernel(seed, student_seed, plane, gain_hbm, student_gain_hbm, out, gain, student_gain, sems):
    start = pl.multiple_of(plane[0] * STEP_Q, STEP_Q)
    copies = [
        pltpu.make_async_copy(gain_hbm, gain, sems.at[0]),
        pltpu.make_async_copy(student_gain_hbm.at[:, pl.ds(start, STEP_Q)], student_gain, sems.at[1]),
    ]
    for copy in copies:
        copy.start()
    for copy in copies:
        copy.wait()
    rows = [gain[:, index * PIECE : (index + 1) * PIECE] for index in range(SEG)]
    for value in (seed[0], student_seed[0]):
        for shift in (16, 8, 0):
            byte = jnp.bitwise_and(lax.shift_right_logical(value, jnp.int32(shift)), jnp.int32(255))
            rows.append(jnp.full((1, PIECE), byte, jnp.int32).astype(F32).astype(BF))
    rows += [jnp.zeros((1, PIECE), BF)] * 2
    for index in range(4 * SEG):
        rows.append(student_gain[:, index * PIECE : (index + 1) * PIECE])
    for first in range(0, FACTS, 16):
        out[first : first + 16, :] = jnp.concatenate([row.astype(F32) for row in rows[first : first + 16]], axis=0).astype(BF)


def chip_kernel(core, own, other, out):
    out[core[0]] = own[...]
    out[1 - core[0]] = other[...]


def facts_kernel(place, student_seed, *refs):
    parts, (along_z_out, along_y_out, even_out, place_out, student_out) = refs[:4], refs[4:9]
    fold_place_out, fold_gain_out, up_place_out, up_gain_out, facts = refs[9:]
    core, column, row, plane = place[1], place[2], place[3], place[4]
    for partner, part in zip(SHORT, parts):
        facts[pl.ds(2 * jnp.bitwise_xor(column, partner), 2)] = part[...].astype(F32)

    def seed(layer, first):
        high, middle, low = (facts[layer, first + index : first + index + 1, :].astype(jnp.int32) for index in range(3))
        return high * 65536 + middle * 256 + low

    for digit in range(4):
        along_z_out[digit] = facts[0, pl.ds(2 * digit + core, 1), :]
        for pair in range(4):
            even_out[pair, digit] = facts[2 * pair, pl.ds(2 * digit + core, 1), :]
    index = lax.broadcasted_iota(jnp.int32, (16, PIECE), 0)
    gains = jnp.zeros((16, PIECE), F32)
    for pair in range(4):
        gains = jnp.where(index == pair, facts[2 * pair + 1, pl.ds(2 * column + core, 1), :], gains)
    along_y_out[...] = gains.astype(BF)
    even = (row * STEP_P + core * STEP_C) * 16411 + plane * STEP_Q + column * STEP_R
    odd = (column * STEP_R + core * STEP_C) * 16411 + plane * STEP_Q + row * STEP_P
    for layer in range(LAYERS):
        place_out[layer : layer + 1, :] = seed(layer, SEG) * 1000003 + (even if layer % 2 == 0 else odd)
    odd_place = (plane * STEP_Q + column * STEP_R + core * STEP_C) * 16411
    fold_place_out[...] = jnp.broadcast_to(seed(LAYERS - 1, SEG + 3) * 1000003 + odd_place, (SEG, PIECE))
    for digit in range(4):
        fold_gain_out[digit] = facts[LAYERS - 1, pl.ds(16 + SEG * digit + place[0], 1), :]
    block = plane * 4 + row
    for half in range(2):
        chip = facts[pl.ds(2 * column + half, 1)][0]
        high, middle, low = (chip[SEG + 3 + index : SEG + 4 + index].astype(jnp.int32) for index in range(3))
        up_seed = high * 65536 + middle * 256 + low
        up_place_out[half] = jnp.broadcast_to(up_seed * 1000003 + block * (WIDTH * 16411), (SEG, PIECE))
        for digit in range(4):
            index = 16 + SEG * row + 2 * digit + core
            up_gain_out[half, digit] = facts[pl.ds(2 * column + half, 1), pl.ds(index, 1), :][0]
    student_out[...] = jnp.full((SEG, PIECE), student_seed[0] * 1000003 + block * (WIDTH * 16411), jnp.int32)


def squares_tile(squares):
    return split_row(jnp.sum(jnp.transpose(squares), axis=0, keepdims=True))


def embed_kernel(place, token, out, tile_out, before_out):
    tokens = jnp.broadcast_to(token[...], (TOK, PIECE)) * 16411 + wrapped(EMBED_KEY * 1000003)
    tokens = tokens + lax.broadcasted_iota(jnp.int32, (TOK, PIECE), 1)
    tokens = tokens + (place[1] * STEP_C + place[3] * STEP_P)
    squares = jnp.zeros((TOK, PIECE), F32)
    for slot, partner in enumerate(PARTNERS):
        for digit in range(4):
            first = jnp.bitwise_xor(place[4], partner) * STEP_Q + digit * STEP_R
            part = hashed(tokens + first, math.sqrt(3.0)).astype(BF)
            out[slot, digit * TOK : (digit + 1) * TOK, :] = part
            wide = part.astype(F32)
            squares = squares + wide * wide
    tile_out[...] = squares_tile(squares)
    tokens = tokens + (place[2] * STEP_R + place[4] * STEP_Q - place[3] * STEP_P)
    for digit in range(4):
        rows = slice(digit * TOK, (digit + 1) * TOK)
        before_out[rows, :] = hashed(tokens + digit * STEP_P, math.sqrt(3.0)).astype(BF)


def first_scale_kernel(embedded, tile, *refs):
    gains, outs = dict(zip(SHORT, refs[:4])), refs[4:]
    for slot, partner in enumerate(PARTNERS):
        for digit in range(4):
            rows = slice(digit * TOK, (digit + 1) * TOK)
            outs[slot][rows, :] = (embedded[slot, rows, :].astype(F32) * gains[partner][digit]).astype(BF)
        outs[slot][STATE:, :] = tile[...] if slot == 0 else jnp.zeros((16, TOK), BF)


def weight_kernel(layer, plane, place, out):
    chunk = 64
    row_step, col_step = (STEP_R, STEP_P) if layer % 2 == 0 else (STEP_P, STEP_R)
    row = lax.broadcasted_iota(jnp.int32, (chunk, WIDTH), 0)
    col = lax.broadcasted_iota(jnp.int32, (chunk, WIDTH), 1)
    col = (col // 512) * STEP_C + (col // PIECE % 4) * col_step + col % PIECE
    base = row * 16411 + col + jnp.concatenate([place[layer : layer + 1, :]] * (WIDTH // PIECE), axis=1)

    def step(index, carry):
        piece = index // 2
        slot = piece // 4
        partner = jnp.where(slot == 0, 0, jnp.where(slot == 1, PARTNERS[1], jnp.where(slot == 2, PARTNERS[2], PARTNERS[3])))
        first = jnp.bitwise_xor(plane[0], partner) * (STEP_Q * 16411) + (piece % 4) * (row_step * 16411) + (index % 2) * (chunk * 16411)
        start = pl.multiple_of(index * chunk, chunk)
        out[pl.ds(start, chunk), :] = hashed(base + first, math.sqrt(3.0 / D)).astype(BF)
        return carry

    lax.fori_loop(0, 2048 // chunk, step, 0, unroll=2)


WEIGHTS = 2048 * WIDTH


def teacher_weight(layer, plane, place):
    body = functools.partial(weight_kernel, layer)
    return call(body, "weight", sds((2048, WIDTH), BF), [SMEM, VMEM], flops=20 * WEIGHTS, nbytes=2 * WEIGHTS)(
        plane, place
    )


def contract_kernel(theirs, core, *refs):
    parts, (weight, *more, out) = refs[:4], refs[4:]
    scaled = [part[digit * TOK : (digit + 1) * TOK, :] for part in parts for digit in range(4)]
    scaled = jnp.concatenate(scaled, axis=1)
    squares = joined_row(parts[0][STATE:, :])
    for part in parts[1:]:
        squares = squares + joined_row(part[STATE:, :])
    out[STATE:GATHER, :] = split_row(squares).astype(out.dtype)
    if more:
        out[GATHER:, :] = more[0][...].astype(out.dtype)
    elif out.shape[0] > GATHER:
        folded = parts[0][GATHER : GATHER + TOK, :].astype(F32)
        for part in parts[1:]:
            folded = folded + part[GATHER : GATHER + TOK, :].astype(F32)
        out[GATHER:, :] = folded.astype(out.dtype)
    first = (1 - core[0] if theirs else core[0]) * STATE
    for pair in range(2):
        columns = pl.ds(pl.multiple_of(first + pair * 256, 256), 256)
        part = jnp.dot(scaled, weight[:, columns], preferred_element_type=F32).astype(out.dtype)
        for half in range(2):
            rows = slice((2 * pair + half) * TOK, (2 * pair + half + 1) * TOK)
            out[rows, :] = part[:, half * PIECE : (half + 1) * PIECE]


def pair_kernel(digit, own, other, stream, *refs):
    *more, out = refs
    total = own[...] + other[...].astype(F32)
    out[:STATE, :] = total[:STATE].astype(BF)
    if more:
        out[STATE:GATHER, :] = split_row(joined_row(total[STATE:GATHER]))
        out[GATHER:, :] = more[0][...]
        return
    start = pl.multiple_of(digit[0] * TOK, TOK)
    out[STATE : STATE + TOK, :] = stream[pl.ds(start, TOK), :]
    out[STATE + TOK : SUM, :] = split_row(joined_row(total[STATE:GATHER]))
    if total.shape[0] > GATHER:
        out[SUM:, :] = total[GATHER:].astype(BF)


def placed(digit, parts, out):
    for partner, part in zip(PARTNERS, parts):
        start = pl.multiple_of(jnp.bitwise_xor(digit[0], partner) * TOK, TOK)
        out[pl.ds(start, TOK), :] = part[STATE : STATE + TOK, :]


def pre_kernel(part_a, part_b, part_c, part_d, out):
    parts = zip(PARTNERS, (part_a, part_b, part_c, part_d))
    wide = {partner: part[GATHER + TOK :, :].astype(F32) for partner, part in parts}
    out[...] = (wide[0] + wide[1]) + (wide[2] + wide[3])


def keep_kernel(digit, part_a, part_b, part_c, part_d, out):
    placed(digit, (part_a, part_b, part_c, part_d), out)


def fold_weight_kernel(place, out):
    base = ternary_base(place)
    for digit in range(4):
        made = ternary(base + digit * (STEP_P * 16411), math.sqrt(1.5 / D))
        out[digit * TOK : (digit + 1) * TOK, :] = made.astype(BF)


def update_kernel(layer, digit, part_a, part_b, part_c, part_d, *refs):
    parts = (part_a, part_b, part_c, part_d)
    following = layer + 1 < LAYERS
    fold = layer + 2 == LAYERS
    if layer == 0:
        before, stream_out, mean_out, message_out, gains = refs
        for partner, part in zip(PARTNERS, parts):
            for index in range(4):
                row = part[GATHER : GATHER + 16, :][index : index + 1].astype(F32)
                gains[index, jnp.bitwise_xor(digit[0], partner)] = row
    elif fold:
        gains, fold_weight, fold_gain, stream_out, mean_out, message_out = refs
    elif following:
        gains, stream_out, mean_out, message_out = refs
    else:
        stream_out, mean_out, odd_out, pre_out = refs
    if layer:
        placed(digit, parts, stream_out)
    else:
        stream_out[...] = before[...]

    def total(rows):
        wide = {partner: part[rows, :].astype(F32) for partner, part in zip(PARTNERS, parts)}
        return (wide[0] + wide[1]) + (wide[2] + wide[3])

    if not following:
        odd_out[...] = stream_out[...]
        pre_out[...] = total(slice(SUM, SUM + TOK))
    squares = joined_row(total(slice(STATE + TOK, SUM) if layer else slice(STATE, GATHER)))
    mean = jnp.transpose(jnp.broadcast_to(squares, (TOK, TOK))) * np.float32(1.0 / D)
    mean_out[...] = mean
    scale = lax.rsqrt(mean + EPSILON)
    squares = jnp.zeros((TOK, PIECE), F32)
    folded = jnp.zeros((TOK, R), F32)
    for index in range(4):
        rows = slice(index * TOK, (index + 1) * TOK)
        result = (stream_out[rows, :].astype(F32) + total(rows) * scale).astype(BF)
        stream_out[rows, :] = result
        if following:
            wide = result.astype(F32)
            squares = squares + wide * wide
            message_out[rows, :] = (wide * gains[(layer + 1) // 2, index]).astype(BF)
        if fold:
            scaled = (wide * fold_gain[index]).astype(BF)
            folded = folded + jnp.dot(scaled, fold_weight[rows, :], preferred_element_type=F32)
    if following:
        message_out[STATE:GATHER, :] = squares_tile(squares)
    if fold:
        message_out[GATHER : GATHER + TOK, :] = folded.astype(BF)
        message_out[GATHER + TOK :, :] = total(slice(SUM, SUM + TOK)).astype(BF)


def select_kernel(column, *refs):
    odd, even = refs[:3], refs[3:7]
    odd_out, now_out, later_out, held = refs[7:]
    for index in range(4):
        held[index] = even[index][...]
        held[5 + index] = odd[min(index, 2)][...]
    held[4] = even[3][...]
    odd_out[...] = held[5 + column[0]]
    now_out[...] = held[column[0]]
    later_out[...] = held[column[0] + 1]


def mean_kernel(segment, *refs):
    means, out = refs[:-1], refs[-1]
    mean = means[0][...]
    for layer in range(1, LAYERS - 1):
        mean = jnp.where(segment[0] == layer, means[layer][...], mean)
    out[...] = mean


def swap_kernel(core, column, odd, last_odd, now, later, last, near_out, mine_out):
    end, first = column[0] == 3, core[0] == 0
    later = jnp.where(end, last[...].astype(F32), later[...].astype(F32))
    now = now[...].astype(F32)
    near_out[:STATE, :] = jnp.where(end, last_odd[...].astype(F32), odd[...].astype(F32)).astype(BF)
    near_out[STATE:, :] = jnp.where(first, later, now).astype(BF)
    mine_out[...] = jnp.where(first, now, later).astype(BF)


CORE = [(i, i ^ 1) for i in range(SEG)]
ALONG = {
    "x": ("segment", 2),
    "y": ("mp", 1),
    "z": ("mp", 4),
}


PARTNERS = (0, 3, 2, 1)
SHORT = (0, 3, 2, 1)


def exchange(values, physical, order=PARTNERS):
    axis, step = ALONG[physical]
    size = SEG if axis == "segment" else MP
    values = values if isinstance(values, (list, tuple)) else [values] * 4
    return [values[0]] + [
        lax.ppermute(values[k], axis, [(i, i ^ (k * step)) for i in range(size)]) for k in order[1:]
    ]


def sum_kernel(*refs):
    parts, out = dict(zip(SHORT, refs[:4])), refs[4]
    own, first, second, third = (parts[k][...].astype(F32) for k in range(4))
    out[...] = ((own + first) + (second + third)).astype(out.dtype)


def summed_along(value, physical, dtype):
    parts = exchange(value, physical, SHORT)
    return call(sum_kernel, "sum", sds(value.shape, dtype), [VMEM] * 4)(*parts)


def ternary_base(place):
    row = lax.broadcasted_iota(jnp.int32, (PIECE, R), 0)
    rank = lax.broadcasted_iota(jnp.int32, (PIECE, R), 1)
    return row * 16411 + rank + place[0:1, :]


def pieces_of(core, index, mine, near, far):
    even = piece_of(core, index, mine, far.at[STATE:])
    odd = piece_of(core, index, near.at[:STATE], far.at[:STATE])
    first = core[0] == 0
    return jnp.where(first, even, odd), jnp.where(first, odd, even)


def piece_of(core, index, here, there):
    first = core[0] == 0
    rows = slice(index // 2 * TOK, (index // 2 + 1) * TOK)
    here, there = here[rows, :].astype(F32), there[rows, :].astype(F32)
    return jnp.where(first, here, there) if index % 2 == 0 else jnp.where(first, there, here)


def student_up_kernel(core, place, gain, now, odd, own_out, other_out):
    totals = []
    for half, stream in enumerate((now, odd)):
        base = ternary_base(place[half]) + core[0] * (STEP_C * 16411)
        total = jnp.zeros((TOK, R), F32)
        for digit in range(4):
            up_weight = ternary(base + digit * (STEP_R * 16411), math.sqrt(1.5 / D)).astype(BF)
            scaled = (stream[digit * TOK : (digit + 1) * TOK, :].astype(F32) * gain[half, digit]).astype(BF)
            total = total + jnp.dot(scaled, up_weight, preferred_element_type=F32)
        totals.append(total)
    first = core[0] == 0
    own_out[...] = jnp.where(first, totals[0], totals[1])
    other_out[...] = jnp.where(first, totals[1], totals[0]).astype(BF)


def down_weight_kernel(place, out):
    base = ternary_base(place) + R
    for index in range(SEG):
        made = ternary(base + index * PIECE * 16411, math.sqrt(1.5 / R))
        out[index * PIECE : (index + 1) * PIECE, :] = made.astype(BF)


def student_error_kernel(
    segment, core, down_weights, mine, near, far, pre, last_pre, mean, last_mean, back_out, scaled_out, squared_out, pre_out
):
    last = segment[0] == SEG - 1
    scale = lax.rsqrt(jnp.where(last, last_mean[...], mean[...]) + EPSILON)
    rectified = jnp.maximum(jnp.where(last, last_pre[...], pre[...]) * scale, 0.0)
    pre_out[...] = rectified
    squared = (rectified * rectified).astype(BF)
    squared_out[...] = squared
    back = jnp.zeros((TOK, R), F32)
    squares = jnp.zeros((TOK, PIECE), F32)
    for index in range(SEG):
        down_weight = down_weights[index * PIECE : (index + 1) * PIECE, :]
        student = lax.dot_general(squared, down_weight, (((1,), (1,)), ((), ())), preferred_element_type=F32)
        given, target = pieces_of(core, index, mine, near, far)
        error = given + student - target
        squares = squares + error * error
        scaled = (error * np.float32(1.0 / TOK)).astype(BF)
        scaled_out[:, index * PIECE : (index + 1) * PIECE] = scaled
        back = back + jnp.dot(scaled, down_weight, preferred_element_type=F32)
    back_out[:TOK, :] = back.astype(BF)
    back_out[TOK:, :] = jnp.sum(squares.reshape(TOK // 16, 16, PIECE), axis=0).astype(BF)


OVER_TOKENS = (((0,), (0,)), ((), ()))


def student_down_kernel(segment, core, mine, near, far, gain, mean, last_mean, scaled, squared, normed_out, down_out):
    scale = lax.rsqrt(jnp.where(segment[0] == SEG - 1, last_mean[...], mean[...]) + EPSILON)
    for index in range(SEG):
        columns = slice(index * PIECE, (index + 1) * PIECE)
        given, _ = pieces_of(core, index, mine, near, far)
        normed = given * scale * gain[:, columns].astype(F32)
        normed_out[columns, :] = jnp.transpose(normed).astype(BF)
    down_out[...] = lax.dot_general(scaled[...], squared[...], OVER_TOKENS, preferred_element_type=F32)


def student_grad_kernel(normed, rectified, back, up_out, loss_out):
    back_pre = (back[:TOK, :] * 2.0 * rectified[...]).astype(BF)
    up_out[...] = jnp.dot(normed[...], back_pre, preferred_element_type=F32)
    total = jnp.sum(jnp.sum(back[TOK:, :], axis=0, keepdims=True), axis=1, keepdims=True)
    loss_out[...] = total * np.float32(1.0 / (TOK * D))


def local(token_ids, teacher_seeds, student_seeds, teacher_gain, student_gain):
    block = lax.axis_index("mp")
    segment = lax.axis_index("segment")
    core, column = lax.rem(segment, 2), segment // 2
    row, plane = lax.rem(block, 4), block // 4
    place = jnp.stack([segment, core, column, row, plane])
    segment, core, column, row, plane = (part.reshape(1) for part in (segment, core, column, row, plane))
    mean_shape = sds((TOK, TOK), F32)
    state_shape = sds((STATE, PIECE), BF)
    gain_shape = sds((4, 1, PIECE), F32)

    pack_scratch = (pltpu.VMEM((1, WIDTH), BF), pltpu.VMEM((1, STEP_Q), BF), pltpu.SemaphoreType.DMA((2,)))
    facts = call(
        pack_kernel, "pack", sds((FACTS, PIECE), BF), [SMEM] * 3 + [HBM] * 2, scratch=pack_scratch
    )(
        teacher_seeds, student_seeds, plane, teacher_gain, student_gain
    )
    facts = call(chip_kernel, "chip", sds((2, FACTS, PIECE), BF), [SMEM, VMEM, VMEM])(
        core, facts, lax.ppermute(facts, "segment", CORE)
    )
    facts = exchange(facts, "x", SHORT)
    embedded, tile, before = call(
        embed_kernel, "embed", (sds((4, STATE, PIECE), BF), sds((16, TOK), BF), state_shape), [SMEM, VMEM]
    )(place, token_ids.reshape(TOK, 1))
    first_gain, odd_gain, even_gains, places, student_place, fold_place, fold_gain, up_place, up_gain = call(
        facts_kernel,
        "facts",
        (gain_shape, sds((16, PIECE), BF), sds((4, 4, 1, PIECE), F32)) + (sds((LAYERS, PIECE), jnp.int32),) * 3
        + (gain_shape, sds((2, SEG, PIECE), jnp.int32), sds((2, 4, 1, PIECE), F32)),
        [SMEM] * 2 + [VMEM] * 4,
        scratch=(pltpu.VMEM((SEG, FACTS, PIECE), F32),),
    )(place, student_seeds, *facts)
    first_gains = exchange(first_gain, "z", SHORT)
    weight = teacher_weight(0, plane, places)
    parts = call(
        first_scale_kernel, "first_scale", tuple(sds((GATHER, PIECE), BF) for _ in range(4)), [VMEM] * 6
    )(embedded, tile, *first_gains)
    streams, odd_halves, means = [embedded[0]], [], []
    student_columns = lax.dynamic_slice_in_dim(student_gain, block * WIDTH, WIDTH, 1)
    for layer in range(LAYERS):
        even = layer % 2 == 0
        (axis, digit), other_digit = (("y", row), column) if even else (("x", column), row)
        last = layer + 1 == LAYERS
        if layer:
            parts = exchange(message, "z")
        if layer in (2, 4, 6):
            *parts, odd_halves[-1] = lax.optimization_barrier((*parts, odd_halves[-1]))
        if last:
            weight = teacher_weight(layer, plane, gate(places, message))
        if layer + 2 == LAYERS:
            odd_half, now, later = call(
                select_kernel,
                "select",
                (state_shape,) * 3,
                [SMEM] + [VMEM] * 7,
                scratch=(pltpu.VMEM((9, STATE, PIECE), BF),),
            )(column, *odd_halves, *streams[0:8:2])
            pre_own, pre_other = call(
                student_up_kernel,
                "student_up",
                (sds((TOK, R), F32), sds((TOK, R), BF)),
                [SMEM] + [VMEM] * 4,
                flops=1 << 25,
            )(core, up_place, up_gain, now, odd_half)
            *parts, pre_own, pre_other = lax.optimization_barrier((*parts, pre_own, pre_other))
        if last:
            mean = call(mean_kernel, "mean", mean_shape, [SMEM] + [VMEM] * 7)(segment, *means)
            *parts, mean = lax.optimization_barrier((*parts, mean))
            pre = call(pre_kernel, "pre", sds((TOK, R), F32), [VMEM] * 4)(*parts)
        rows = GATHER + (TOK if layer + 2 >= LAYERS else 0)
        extra = ([pre_other], [pre_own]) if layer + 2 == LAYERS else ([], [])
        contract = dict(in_specs=[SMEM] + [VMEM] * (5 + len(extra[0])), flops=TOK * WEIGHTS, nbytes=2 * WEIGHTS)
        other = call(functools.partial(contract_kernel, True), "contract_other", sds((rows, PIECE), BF), **contract)(
            core, *parts, weight, *extra[0]
        )
        own = call(functools.partial(contract_kernel, False), "contract_own", sds((rows, PIECE), F32), **contract)(
            core, *parts, weight, *extra[1]
        )
        other = lax.ppermute(other, "segment", CORE)
        more = [odd_gain] if layer == 0 else []
        rows = GATHER + 16 if layer == 0 else SUM + (TOK if layer + 2 >= LAYERS else 0)
        summed = call(pair_kernel, "pair", sds((rows, PIECE), BF), [SMEM] + [VMEM] * (3 + len(more)))(
            other_digit, own, other, streams[-1], *more
        )
        parts = exchange(summed, axis)
        out = [state_shape, mean_shape]
        given = [before] if layer == 0 else [] if last else [odd_gains if even else even_gains]
        if layer + 2 < LAYERS:
            weight = teacher_weight(layer + 1, plane, gate(places, summed))
            *parts, weight = lax.optimization_barrier((*parts, weight))
        if layer + 2 == LAYERS:
            fold_weight = call(fold_weight_kernel, "fold_weight", state_shape, [VMEM])(gate(fold_place, summed))
            *parts, fold_weight = lax.optimization_barrier((*parts, fold_weight))
            given += [fold_weight, fold_gain]
            out.append(sds((GATHER + 2 * TOK, PIECE), BF))
        elif not last:
            out.append(sds((GATHER, PIECE), BF))
        else:
            down_weight = call(down_weight_kernel, "down_weight", sds((WIDTH, R), BF), [VMEM])(
                gate(student_place, summed)
            )
            *parts, down_weight = lax.optimization_barrier((*parts, down_weight))
            out += [state_shape, sds((TOK, R), F32)]
        if layer == 0:
            out.append(sds((4, 4, 1, PIECE), F32))
        stream, stream_mean, *results = call(
            functools.partial(update_kernel, layer), "update", tuple(out), [SMEM] + [VMEM] * (4 + len(given))
        )(digit, *parts, *given)
        if layer in (1, 3, 5):
            odd_halves.append(call(keep_kernel, "keep", state_shape, [SMEM] + [VMEM] * 4)(digit, *parts))
        streams.append(stream)
        if last:
            last_mean, (last_odd, last_pre) = stream_mean, results
        else:
            means.append(stream_mean)
            message = results[0]
        if layer == 0:
            odd_gains = results[1]

    near, mine = call(swap_kernel, "swap", (sds((2 * STATE, PIECE), BF), state_shape), [SMEM] * 2 + [VMEM] * 5)(
        core, column, odd_half, last_odd, now, later, streams[LAYERS]
    )
    far = lax.ppermute(near, "segment", CORE)
    back, scaled, squared, rectified = call(
        student_error_kernel,
        "student_error",
        (sds((TOK + 16, R), BF), sds((TOK, WIDTH), BF), sds((TOK, R), BF), sds((TOK, R), F32)),
        [SMEM] * 2 + [VMEM] * 8,
    )(segment, core, down_weight, mine, near, far, pre, last_pre, mean, last_mean)
    normed, grad_down = call(
        student_down_kernel, "student_down", (sds((WIDTH, TOK), BF), sds((WIDTH, R), F32)), [SMEM] * 2 + [VMEM] * 8
    )(segment, core, mine, near, far, student_columns, mean, last_mean, scaled, squared)
    back = summed_along(summed_along(back, "y", BF), "z", F32)
    grad_up, loss = call(
        student_grad_kernel, "student_grad", (sds((WIDTH, R), F32), sds((1, 1), F32)), [VMEM] * 3
    )(normed, rectified, back)
    return loss.reshape(1), grad_up[None], grad_down[None]


def solution(mesh):
    in_specs = (P(), P("segment"), P("segment"), P("segment", "mp"), P("segment", None))
    out_specs = (P("segment"), P("segment", "mp", None), P("segment", "mp", None))
    return jax.shard_map(local, mesh=mesh, in_specs=in_specs, out_specs=out_specs, check_vma=False)
```
